512 devices in a mesh: chan: 32 (over z_lo, y, core), tm: 16 (over x, z_hi).
Axes of the slice: x: 4, y: 4, z: 16 (z_hi: 4, z_lo: 4; z = z_hi * 4 + z_lo), core: 2. Of those that a mesh axis runs over, the one named last changes fastest.
Arguments:
- samples: bfloat16 [32, 2, 1024, 4096], P('chan', None, None, 'tm')
- feed_flags: int32 [32, 1024], P('chan'), may hold values 0 or 1
- cal_channel: int32 [16], replicated, may hold values from 0 to 31, as said below
- gain_state: float32 [32, 2, 2, 1024], P('chan', None, None, 'tm'), may hold values from -6 to 6
Outputs:
- calibrated: bfloat16 [32, 1024, 2, 1024], P('chan', 'tm')
- new_gains: float32 [32, 2, 2, 1024], P('chan', None, None, 'tm')
The draws below stay inside these ranges and needn't reach their ends.
Inputs may be any that keep to these rules, and one draw needn't show every extreme that they name: `cal_channel`: entry p is 2 p or 2 p + 1; entry 0 is 1.
All inputs are finite; a program needn't handle non-finite values. No bound on the sum of `feed_flags` on one device may be relied on, other than what follows from the above.
Results may differ from the reference program's by a relative error of at most 0.017.
Values may be sent and summed in bfloat16 or wider, within the bound.
No kernel may reach another device: no remote copies, remote signals or barrier semaphores. Data moves between devices by JAX's collectives and lax.ppermute only.
A program may use at most 64 MiB of HBM per device.

```python
import math
import jax
import jax.numpy as jnp
from jax import lax

F = 1024
TIME_DEV = 256
ITERS = 8
CHANNELS = 32
PAIRS = 16
TIME = 4096
N_TM = 16


def draw_samples(key, part):
    key = jax.random.fold_in(key, 11)
    key_feed, key_wave, key_noise = jax.random.split(key, 3)
    edge = (1.0 + math.sqrt(F / TIME)) ** 2
    amplitude = jnp.sqrt(jnp.array([2.0, 1.35], jnp.float32) * edge / (2.0 * F))
    rise = 4.0
    noise = jax.random.normal(key_noise, (CHANNELS, 2, F, TIME), jnp.float32)
    positions = jnp.arange(F).astype(jnp.float32) / F
    profile = jnp.exp(0.5 * math.log(rise) * positions)
    feed_gain = jax.random.normal(key_feed, (CHANNELS, 2, 2, F), jnp.float32) * amplitude[None, None, :, None]
    feed_gain = feed_gain * profile[None, None, None, :]
    wave = jax.random.normal(key_wave, (CHANNELS, 2, 2, TIME), jnp.float32)
    real_sum = noise[:, 0]
    imag_sum = noise[:, 1]
    for mode in range(2):
        gain_real = feed_gain[:, 0, mode, :, None]
        gain_imag = feed_gain[:, 1, mode, :, None]
        wave_real = wave[:, 0, mode, None, :]
        wave_imag = wave[:, 1, mode, None, :]
        real_sum = real_sum + gain_real * wave_real - gain_imag * wave_imag
        imag_sum = imag_sum + gain_real * wave_imag + gain_imag * wave_real
    return jnp.stack([real_sum, imag_sum], 1).astype(jnp.bfloat16)


def draw_cal_channel(key, part):
    key = jax.random.fold_in(key, 5)
    choose = jax.random.randint(key, (PAIRS,), 0, 2).astype(jnp.int32)
    choose = jnp.where(jnp.arange(PAIRS) == 0, 1, choose).astype(jnp.int32)
    return (2 * jnp.arange(PAIRS).astype(jnp.int32) + choose).astype(jnp.int32)


def with_ends(result, rng, smallest, high):
    longest = result.shape.index(max(result.shape))
    spots = []
    for shift in (0, 1):
        where = [jax.random.randint(jax.random.fold_in(rng, axis), (), 0, length) for axis, length in enumerate(result.shape)]
        where[longest] = (where[longest] + shift) % result.shape[longest]
        spots.append(tuple(where))
    return result.at[spots[0]].set(smallest).at[spots[1]].set(high)


def levels(own_key, dims, cuts, low, largest):
    level, own = 1.0, jax.random.fold_in(own_key, 6)
    for dim, blocks in cuts:
        steps = jnp.exp(jax.random.uniform(jax.random.fold_in(own, dim), (blocks,), jnp.float32, low / len(cuts), largest / len(cuts)))
        level = level * jnp.repeat(steps, dims[dim] // blocks).reshape([-1 if axis == dim else 1 for axis in range(len(dims))])
    return level


def centred(rng, extent, scale, bound, cuts=(), dtype=jnp.bfloat16):
    drawn = jax.random.normal(rng, extent, jnp.float32) * scale
    if len(cuts) > 0:
        drawn = levels(rng, extent, cuts, -0.22, 0.18) * drawn
    return jnp.clip(drawn, min=-bound, max=bound).astype(dtype)


def setup_inputs(seed: int = 0) -> dict:
    seeds = jax.random.split(jax.random.key(seed), 5)
    return {
        "samples": draw_samples(jax.random.fold_in(seeds[4], 71), 0),
        "feed_flags": with_ends((jax.random.randint(seeds[1], (CHANNELS, F), 0, 8) < 7).astype(jnp.int32), jax.random.fold_in(seeds[1], 1), 0, 1),
        "cal_channel": draw_cal_channel(jax.random.fold_in(seeds[4], 71), 0),
        "gain_state": centred(seeds[3], (CHANNELS, 2, 2, F), 1.0, 6.0, ((0, 32), (3, 16)), jnp.float32),
    }


epsilon = 1e-06
smoothing = 0.75

def shard_partial(pieces):
    real_part = pieces[0]
    imag_part = pieces[1]
    feeds = real_part.shape[0]
    width = real_part.shape[1]
    paired = jnp.stack([jnp.concatenate([real_part, imag_part], 1), jnp.concatenate([imag_part, -real_part], 1)], 1)
    left_side = paired.reshape(2 * feeds, 2 * width)
    right_side = jnp.concatenate([real_part, imag_part], 1)
    product = jnp.dot(left_side, right_side.T, precision=lax.Precision.HIGHEST, preferred_element_type=jnp.float32)
    return product.reshape(feeds, 2, feeds) / TIME

def channel_visibility(inputs):
    channel_samples, channel_flags = inputs
    masked = (channel_samples * channel_flags[None, :, None].astype(jnp.bfloat16)).astype(jnp.float32)

    def accumulate(shard_index, running):
        pieces = lax.dynamic_slice_in_dim(masked, shard_index * TIME_DEV, TIME_DEV, 2)
        rounded = lax.optimization_barrier(shard_partial(pieces).astype(jnp.bfloat16))
        return running + rounded.astype(jnp.float32)
    return lax.fori_loop(0, N_TM, accumulate, jnp.zeros((F, 2, F), jnp.float32))

def start_basis(feeds):
    positions = jnp.arange(feeds).astype(jnp.float32)
    modes = jnp.arange(1, 3).astype(jnp.float32)
    angles = 2.0 * jnp.pi * modes[:, None] * positions[None, :] / feeds
    factor = 1.0 / jnp.sqrt(jnp.ones((), jnp.float32) * feeds)
    return jnp.stack([jnp.cos(angles), jnp.sin(angles)]) * factor

def highest(left_side, right_side):
    return jnp.dot(left_side, right_side, precision=lax.Precision.HIGHEST, preferred_element_type=jnp.float32)

def subspace_gains(cal_block):
    real_block = cal_block[:, 0, :]
    imag_block = cal_block[:, 1, :]
    feeds = cal_block.shape[2]
    basis = start_basis(feeds)
    for sweep in range(ITERS):
        zeta_real = highest(real_block, basis[0].T) - highest(imag_block, basis[1].T)
        zeta_imag = highest(real_block, basis[1].T) + highest(imag_block, basis[0].T)
        one_real, two_real = (zeta_real[:, 0], zeta_real[:, 1])
        one_imag, two_imag = (zeta_imag[:, 0], zeta_imag[:, 1])
        first_norm = jnp.sqrt(epsilon + jnp.sum(one_real * one_real + one_imag * one_imag))
        cross_real = jnp.sum(one_real * two_real + one_imag * two_imag) / first_norm
        cross_imag = jnp.sum(one_real * two_imag - one_imag * two_real) / first_norm
        rest_real = two_real - (one_real * cross_real - one_imag * cross_imag) / first_norm
        rest_imag = two_imag - (one_real * cross_imag + one_imag * cross_real) / first_norm
        second_norm = jnp.sqrt(epsilon + jnp.sum(rest_real * rest_real + rest_imag * rest_imag))
        basis = jnp.stack([jnp.stack([one_real / first_norm, rest_real / second_norm]), jnp.stack([one_imag / first_norm, rest_imag / second_norm])])
    weights = jnp.sqrt(jnp.stack([first_norm, second_norm]) * feeds)
    return basis * weights[None, :, None]

def reference(samples, feed_flags, cal_channel, gain_state):
    visibility = lax.map(channel_visibility, (samples, feed_flags))

    def channel_result(inputs):
        channel_index, channel_state, channel_vis = inputs
        cal_block = visibility[cal_channel[channel_index // 2]]
        solved = subspace_gains(cal_block)
        gains_now = smoothing * channel_state + (1.0 - smoothing) * solved
        power = lax.optimization_barrier(jnp.sum(gains_now * gains_now, axis=(0, 1)))
        mean_power = jnp.mean(power)
        scale = jnp.sqrt((mean_power + epsilon) / (power + mean_power + epsilon))
        calibrated = (channel_vis * scale[:, None, None] * scale[None, None, :]).astype(jnp.bfloat16)
        return (calibrated, gains_now)
    return lax.map(channel_result, (jnp.arange(CHANNELS).astype(jnp.int32), gain_state, visibility))
```

```python
import functools, math
import numpy as np
import jax
import jax.numpy as jnp
from jax import lax
from jax.experimental import pallas as pl
from jax.experimental.pallas import tpu as pltpu
from jax.sharding import PartitionSpec as P

ITERS = 8
epsilon = 1e-06
smoothing = 0.75

def gram_kernel(scale, samples_ref, flags_ref, out_ref, left, right):
    feeds, width = samples_ref.shape[1:]
    block = out_ref.shape[0]
    step = pl.program_id(0)

    @pl.when(step == 0)
    def _():
        good = jnp.broadcast_to(flags_ref[...].astype(jnp.float32), (128, feeds)).T
        good = jnp.concatenate([good] * (width // 128), 1).astype(jnp.bfloat16)
        re = samples_ref[0] * good
        im = samples_ref[1] * good
        right[:, :width] = re
        right[:, width:] = im
        left[:, :width] = im
        left[:, width:] = -re

    rows = pl.ds(pl.multiple_of(step * block, block), block)
    nt = (((1,), (1,)), ((), ()))
    total = lax.dot_general(right[rows, :], right[...], nt, preferred_element_type=jnp.float32)
    total += lax.dot_general(left[rows, :], right[...], nt, preferred_element_type=jnp.float32)
    out_ref[...] = (total * scale).astype(jnp.bfloat16)

def gram(samples, flags, all_time):
    _, feeds, width = samples.shape
    blocks = 4
    return pl.pallas_call(
        functools.partial(gram_kernel, 1.0 / all_time),
        grid=(blocks,),
        out_shape=jax.ShapeDtypeStruct((feeds, feeds), jnp.bfloat16),
        in_specs=[pl.BlockSpec((2, feeds, width), lambda i: (0, 0, 0)), pl.BlockSpec((1, feeds), lambda i: (0, 0))],
        out_specs=pl.BlockSpec((feeds // blocks, feeds), lambda i: (i, 0)),
        scratch_shapes=[pltpu.VMEM((feeds, 2 * width), jnp.bfloat16)] * 2,
        compiler_params=pltpu.CompilerParams(vmem_limit_bytes=40 << 20),
        name="gram",
    )(samples, flags)

def basis_rows(feeds):
    f = np.arange(feeds, dtype=np.float64)
    ang = 2 * np.pi * np.arange(1, 3)[:, None] * f / feeds
    return (np.concatenate([np.cos(ang), np.sin(ang)]) / math.sqrt(feeds)).astype(np.float32)

def split3(v):
    hi = v.astype(jnp.bfloat16)
    rest = v - hi.astype(jnp.float32)
    mid = rest.astype(jnp.bfloat16)
    lo = (rest - mid.astype(jnp.float32)).astype(jnp.bfloat16)
    return hi, mid, lo

def total(v):
    return jnp.sum(v, axis=1, keepdims=True)

def solve_kernel(parity_ref, own_ref, other_ref, basis_ref, state_ref, gains_ref, scale_ref, mat, mat_t):
    feeds = mat.shape[0]
    parity = parity_ref[0]
    half = 32
    for s in range(feeds // (2 * half)):
        mat[pl.ds(pl.multiple_of(2 * half * s + half * parity, half), half), :] = own_ref[half * s:half * (s + 1), :]
        mat[pl.ds(pl.multiple_of(2 * half * s + half * (1 - parity), half), half), :] = other_ref[half * s:half * (s + 1), :]
    for i in range(feeds // 256):
        mat_t[:, 256 * i:256 * (i + 1)] = mat[256 * i:256 * (i + 1), :].T

    def sweep(_, carry):
        qr, qi, _, _ = carry
        s4 = jnp.concatenate([qr + qi, qr - qi], 0)
        hi, mid, lo = split3(s4)
        left = jnp.concatenate([hi, mid, lo, jnp.zeros_like(hi)], 0)
        with_t = jnp.dot(left, mat_t[...], preferred_element_type=jnp.float32)
        with_m = jnp.dot(left, mat[...], preferred_element_type=jnp.float32)
        with_t = (with_t[0:4] + with_t[4:8]) + with_t[8:12]
        with_m = (with_m[0:4] + with_m[4:8]) + with_m[8:12]
        zr = 0.5 * (with_t[2:4] + with_m[0:2])
        zi = 0.5 * (with_t[0:2] - with_m[2:4])
        one_r, two_r = zr[0:1], zr[1:2]
        one_i, two_i = zi[0:1], zi[1:2]
        n1 = total(one_r * one_r + one_i * one_i)
        cr = total(one_r * two_r + one_i * two_i)
        ci = total(one_r * two_i - one_i * two_r)
        first = jnp.sqrt(epsilon + n1)
        cr = cr / first
        ci = ci / first
        rest_r = two_r - (one_r * cr - one_i * ci) / first
        rest_i = two_i - (one_r * ci + one_i * cr) / first
        second = jnp.sqrt(epsilon + total(rest_r * rest_r + rest_i * rest_i))
        qr = jnp.concatenate([one_r / first, rest_r / second], 0)
        qi = jnp.concatenate([one_i / first, rest_i / second], 0)
        return qr, qi, first, second

    one = jnp.ones((1, 1), jnp.float32)
    qr, qi, first, second = lax.fori_loop(0, ITERS, sweep, (basis_ref[0:2], basis_ref[2:4], one, one))
    weights = jnp.concatenate([jnp.sqrt(first * feeds), jnp.sqrt(second * feeds)], 0)
    solved = jnp.concatenate([qr * weights, qi * weights], 0)
    gains = smoothing * state_ref[...] + (1.0 - smoothing) * solved
    gains_ref[...] = gains
    power = jnp.sum(gains * gains, axis=0, keepdims=True)
    mean_power = total(power) / feeds
    scale_ref[...] = jnp.sqrt((mean_power + epsilon) / (power + mean_power + epsilon))

def solve(parity, own, other, state):
    feeds = own.shape[1]
    vm = pl.BlockSpec(memory_space=pltpu.VMEM)
    return pl.pallas_call(
        solve_kernel,
        out_shape=(jax.ShapeDtypeStruct((4, feeds), jnp.float32), jax.ShapeDtypeStruct((1, feeds), jnp.float32)),
        in_specs=[pl.BlockSpec(memory_space=pltpu.SMEM), vm, vm, vm, vm],
        out_specs=(vm, vm),
        scratch_shapes=[pltpu.VMEM((feeds, feeds), jnp.bfloat16)] * 2,
        compiler_params=pltpu.CompilerParams(vmem_limit_bytes=40 << 20),
        name="solve",
    )(parity, own, other, jnp.asarray(basis_rows(feeds)), state)


def groups(mesh_shape_x, mesh_shape_z):
    along_x = [[x * mesh_shape_z + z for x in range(mesh_shape_x)] for z in range(mesh_shape_z)]
    along_z = [[x * mesh_shape_z + z for z in range(mesh_shape_z)] for x in range(mesh_shape_x)]
    return along_x, along_z


def exchange(value, which):
    return lax.all_to_all(value, "tm", 0, 0, axis_index_groups=which)


def swap_cores(value):
    count = lax.axis_size("chan")
    return lax.ppermute(value, "chan", [(i, i ^ 1) for i in range(count)])


def on_device(samples, feed_flags, cal_channel, gain_state):
    feeds = samples.shape[2]
    tm_count = lax.axis_size("tm")
    nx = nz = 4
    along_x, along_z = groups(nx, nz)
    rows = feeds // tm_count
    half = rows // 2
    tm = lax.axis_index("tm")
    chan = lax.axis_index("chan")
    parity = chan % 2
    f32, bf16 = jnp.float32, jnp.bfloat16

    state = lax.all_gather(gain_state[0], "tm", axis=2, tiled=True).reshape(4, feeds)
    packed = gram(samples[0], feed_flags, samples.shape[3] * tm_count)

    part = exchange(packed.reshape(nx, nz * rows, feeds), along_x)
    part = jnp.sum(part.astype(f32), axis=0).astype(bf16)
    part = exchange(part.reshape(nz, rows, feeds), along_z)
    mine = jnp.sum(part.astype(f32), axis=0)
    sent = mine.astype(bf16)

    is_cal = cal_channel[chan // 2] == chan
    keep = lax.dynamic_slice_in_dim(sent, parity * half, half, 0)
    give = lax.dynamic_slice_in_dim(sent, (1 - parity) * half, half, 0)
    cal_rows = jnp.where(is_cal, keep, swap_cores(give))

    mirror = sent.reshape(rows, nx, nz, rows).transpose(2, 0, 1, 3)
    mirror = mirror.reshape(nz, 4, rows // 4, nx * rows).transpose(0, 2, 1, 3).reshape(nz, rows // 4, feeds)
    payload = jnp.concatenate([jnp.broadcast_to(cal_rows[None], (nz, half, feeds)), mirror], 1)
    got = exchange(payload, along_z)
    cal_rows = got[:, :half].reshape(nz * half, feeds)
    mirror = got[:, half:].reshape(nz, rows // 4, 4, nx * rows).transpose(0, 2, 1, 3).reshape(nz * rows, nx * rows)
    mirror = mirror.T.reshape(nx, 4, rows // 4, nz * rows).transpose(0, 2, 1, 3).reshape(nx, rows // 4, feeds)
    payload = jnp.concatenate([jnp.broadcast_to(cal_rows[None], (nx, nz * half, feeds)), mirror], 1)
    got = exchange(payload, along_x)
    own = got[:, : nz * half].reshape(feeds // 2, feeds)
    other = swap_cores(own)
    mirror = got[:, nz * half :].reshape(nx, rows // 4, 4, nz * rows).transpose(2, 1, 0, 3).reshape(rows, feeds)

    gains, scale = solve(parity.reshape(1).astype(jnp.int32), own, other, state)
    gains_now = lax.dynamic_slice_in_dim(gains, tm * rows, rows, 1).reshape(1, 2, 2, rows)
    scale_rows = lax.dynamic_slice_in_dim(scale[0], tm * rows, rows, 0)
    mirror = mirror.astype(f32)
    both = 0.5 * jnp.stack([mine + mirror, mine - mirror], 1)
    calibrated = (both * scale_rows[:, None, None] * scale[0][None, None, :]).astype(bf16)
    return (calibrated[None], gains_now)


def solution(mesh):
    return jax.shard_map(
        on_device,
        mesh=mesh,
        in_specs=(P("chan", None, None, "tm"), P("chan", None), P(), P("chan", None, None, "tm")),
        out_specs=(P("chan", "tm", None, None), P("chan", None, None, "tm")),
        check_vma=False,
    )
```

```python
import functools, math
import numpy as np
import jax
import jax.numpy as jnp
from jax import lax
from jax.experimental import pallas as pl
from jax.experimental.pallas import tpu as pltpu
from jax.sharding import PartitionSpec as P

ITERS = 8
epsilon = 1e-06
smoothing = 0.75

def gram_kernel(scale, samples_ref, flags_ref, out_ref, left, right):
    feeds, width = samples_ref.shape[1:]
    block = out_ref.shape[0]
    step = pl.program_id(0)

    @pl.when(step == 0)
    def _():
        good = jnp.broadcast_to(flags_ref[...].astype(jnp.float32), (128, feeds)).T
        good = jnp.concatenate([good] * (width // 128), 1).astype(jnp.bfloat16)
        re = samples_ref[0] * good
        im = samples_ref[1] * good
        right[:, :width] = re
        right[:, width:] = im
        left[:, :width] = im
        left[:, width:] = -re

    rows = pl.ds(pl.multiple_of(step * block, block), block)
    nt = (((1,), (1,)), ((), ()))
    total = lax.dot_general(right[rows, :], right[...], nt, preferred_element_type=jnp.float32)
    total += lax.dot_general(left[rows, :], right[...], nt, preferred_element_type=jnp.float32)
    out_ref[...] = (total * scale).astype(jnp.bfloat16)

def gram(samples, flags, all_time):
    _, feeds, width = samples.shape
    blocks = 4
    return pl.pallas_call(
        functools.partial(gram_kernel, 1.0 / all_time),
        grid=(blocks,),
        out_shape=jax.ShapeDtypeStruct((feeds, feeds), jnp.bfloat16),
        in_specs=[pl.BlockSpec((2, feeds, width), lambda i: (0, 0, 0)), pl.BlockSpec((1, feeds), lambda i: (0, 0))],
        out_specs=pl.BlockSpec((feeds // blocks, feeds), lambda i: (i, 0)),
        scratch_shapes=[pltpu.VMEM((feeds, 2 * width), jnp.bfloat16)] * 2,
        compiler_params=pltpu.CompilerParams(vmem_limit_bytes=40 << 20),
        name="gram",
    )(samples, flags)

def basis_rows(feeds):
    f = np.arange(feeds, dtype=np.float64)
    ang = 2 * np.pi * np.arange(1, 3)[:, None] * f / feeds
    return (np.concatenate([np.cos(ang), np.sin(ang)]) / math.sqrt(feeds)).astype(np.float32)

def split3(v):
    hi = v.astype(jnp.bfloat16)
    rest = v - hi.astype(jnp.float32)
    mid = rest.astype(jnp.bfloat16)
    lo = (rest - mid.astype(jnp.float32)).astype(jnp.bfloat16)
    return hi, mid, lo

def total(v):
    return jnp.sum(v, axis=1, keepdims=True)

def solve_kernel(place_ref, own_ref, basis_ref, solved_ref, mirror_ref, mat_t):
    feeds = own_ref.shape[0]
    rows = mirror_ref.shape[0]
    for i in range(feeds // 256):
        mat_t[:, 256 * i:256 * (i + 1)] = own_ref[256 * i:256 * (i + 1), :].T
    mirror_ref[...] = mat_t[pl.ds(pl.multiple_of(place_ref[0] * rows, rows), rows), :]

    def sweep(_, carry):
        qr, qi, _, _ = carry
        s4 = jnp.concatenate([qr + qi, qr - qi], 0)
        hi, mid, lo = split3(s4)
        left = jnp.concatenate([hi, mid, lo, jnp.zeros_like(hi)], 0)
        with_t = jnp.dot(left, mat_t[...], preferred_element_type=jnp.float32)
        with_m = jnp.dot(left, own_ref[...], preferred_element_type=jnp.float32)
        with_t = (with_t[0:4] + with_t[4:8]) + with_t[8:12]
        with_m = (with_m[0:4] + with_m[4:8]) + with_m[8:12]
        zr = 0.5 * (with_t[2:4] + with_m[0:2])
        zi = 0.5 * (with_t[0:2] - with_m[2:4])
        one_r, two_r = zr[0:1], zr[1:2]
        one_i, two_i = zi[0:1], zi[1:2]
        n1 = total(one_r * one_r + one_i * one_i)
        cr = total(one_r * two_r + one_i * two_i)
        ci = total(one_r * two_i - one_i * two_r)
        first = jnp.sqrt(epsilon + n1)
        cr = cr / first
        ci = ci / first
        rest_r = two_r - (one_r * cr - one_i * ci) / first
        rest_i = two_i - (one_r * ci + one_i * cr) / first
        second = jnp.sqrt(epsilon + total(rest_r * rest_r + rest_i * rest_i))
        qr = jnp.concatenate([one_r / first, rest_r / second], 0)
        qi = jnp.concatenate([one_i / first, rest_i / second], 0)
        return qr, qi, first, second

    one = jnp.ones((1, 1), jnp.float32)
    qr, qi, first, second = lax.fori_loop(0, ITERS, sweep, (basis_ref[0:2], basis_ref[2:4], one, one))
    weights = jnp.concatenate([jnp.sqrt(first * feeds), jnp.sqrt(second * feeds)], 0)
    solved_ref[...] = jnp.concatenate([qr * weights, qi * weights], 0)


def solve(place, own, rows):
    feeds = own.shape[1]
    vm = pl.BlockSpec(memory_space=pltpu.VMEM)
    return pl.pallas_call(
        solve_kernel,
        out_shape=(jax.ShapeDtypeStruct((4, feeds), jnp.float32), jax.ShapeDtypeStruct((rows, feeds), jnp.bfloat16)),
        in_specs=[pl.BlockSpec(memory_space=pltpu.SMEM), vm, vm],
        out_specs=(vm, vm),
        scratch_shapes=[pltpu.VMEM((feeds, feeds), jnp.bfloat16)],
        compiler_params=pltpu.CompilerParams(vmem_limit_bytes=40 << 20),
        name="solve",
    )(place, own, jnp.asarray(basis_rows(feeds)))


def rescale_kernel(place_ref, cal_ref, kept_ref, swapped_ref, state_ref, mine_ref, mirror_ref,
                   gains_ref, out_ref, turned):
    feeds = mine_ref.shape[1]
    rows = mine_ref.shape[0]
    place = place_ref[0]
    is_cal = cal_ref[0] > 0
    solved = jnp.where(is_cal, kept_ref[...], swapped_ref[...])
    state = jnp.where(is_cal, swapped_ref[...], state_ref[...])
    gains = smoothing * state + (1.0 - smoothing) * solved
    gains_ref[...] = gains
    power = jnp.sum(gains * gains, axis=0, keepdims=True)
    mean_power = total(power) / feeds
    scale = jnp.sqrt((mean_power + epsilon) / (power + mean_power + epsilon))
    turned[...] = jnp.broadcast_to(scale, (128, feeds)).T
    down = turned[pl.ds(pl.multiple_of(place * rows, rows), rows), :]
    down = jnp.concatenate([down] * (feeds // 128), 1)
    factor = 0.5 * (down * scale)
    mine = mine_ref[...]
    mirror = mirror_ref[...].astype(jnp.float32)
    out_ref[0] = ((mine + mirror) * factor).astype(jnp.bfloat16)
    out_ref[1] = ((mine - mirror) * factor).astype(jnp.bfloat16)


def rescale(place, cal, kept, swapped, state, mine, mirror):
    rows, feeds = mine.shape
    vm = pl.BlockSpec(memory_space=pltpu.VMEM)
    sm = pl.BlockSpec(memory_space=pltpu.SMEM)
    return pl.pallas_call(
        rescale_kernel,
        out_shape=(jax.ShapeDtypeStruct((4, feeds), jnp.float32), jax.ShapeDtypeStruct((2, rows, feeds), jnp.bfloat16)),
        in_specs=[sm, sm] + [vm] * 5,
        out_specs=(vm, vm),
        scratch_shapes=[pltpu.VMEM((feeds, 128), jnp.float32)],
        compiler_params=pltpu.CompilerParams(vmem_limit_bytes=40 << 20),
        name="rescale",
    )(place, cal, kept, swapped, state, mine, mirror)


def groups(mesh_shape_x, mesh_shape_z):
    along_x = [[x * mesh_shape_z + z for x in range(mesh_shape_x)] for z in range(mesh_shape_z)]
    along_z = [[x * mesh_shape_z + z for z in range(mesh_shape_z)] for x in range(mesh_shape_x)]
    return along_x, along_z


def exchange(value, which):
    return lax.all_to_all(value, "tm", 0, 0, axis_index_groups=which)


def swap_cores(value):
    count = lax.axis_size("chan")
    return lax.ppermute(value, "chan", [(i, i ^ 1) for i in range(count)])


def on_device(samples, feed_flags, cal_channel, gain_state):
    feeds = samples.shape[2]
    tm_count = lax.axis_size("tm")
    nx = nz = 4
    along_x, along_z = groups(nx, nz)
    rows = feeds // tm_count
    thin = rows // nz
    tm = lax.axis_index("tm")
    chan = lax.axis_index("chan")
    f32, bf16 = jnp.float32, jnp.bfloat16
    place = tm.reshape(1).astype(jnp.int32)
    is_cal = cal_channel[chan // 2] == chan
    samples, feed_flags, is_cal, place = lax.optimization_barrier((samples, feed_flags, is_cal, place))
    cal = is_cal.reshape(1).astype(jnp.int32)

    packed = gram(samples[0], feed_flags, samples.shape[3] * tm_count)
    packed, own_state = lax.optimization_barrier((packed, gain_state[0].reshape(4, rows)))
    part = exchange(packed.reshape(nx, nz * rows, feeds), along_x)
    other_state = swap_cores(own_state)
    part, other_state = lax.optimization_barrier((part, other_state))
    part = jnp.sum(part.astype(f32), axis=0).astype(bf16)
    part = exchange(part.reshape(nz, rows, feeds), along_z)
    part, states = lax.optimization_barrier((part, jnp.concatenate([own_state, other_state], 0)))
    mine = jnp.sum(part.astype(f32), axis=0)
    sent = mine.astype(bf16)

    def with_cal(_):
        got = exchange(jnp.broadcast_to(sent[None], (nz, rows, feeds)), along_z)
        got = exchange(jnp.broadcast_to(got.reshape(1, nz * rows, feeds), (nx, nz * rows, feeds)), along_x)
        solved, mirror = solve(place, got.reshape(feeds, feeds), rows)
        return solved, jnp.zeros((4, feeds), f32), mirror

    def without(_):
        high = states.astype(bf16)
        low = (states - high.astype(f32)).astype(bf16)
        halves = jnp.concatenate([high, low], 0)
        halves = jnp.broadcast_to(jnp.pad(halves, ((0, 0), (0, feeds - rows)))[None], (nz, 16, feeds))
        mirror = sent.reshape(rows, nx, nz, rows).transpose(2, 0, 1, 3)
        mirror = mirror.reshape(nz, 4, thin, nx * rows).transpose(0, 2, 1, 3).reshape(nz, thin, feeds)
        got = exchange(jnp.concatenate([mirror, halves], 1), along_z)
        halves = got[:, thin:, :rows].transpose(1, 0, 2).reshape(16, nz * rows)
        halves = jnp.broadcast_to(jnp.pad(halves, ((0, 0), (0, feeds - nz * rows)))[None], (nx, 16, feeds))
        mirror = got[:, :thin].reshape(nz, thin, 4, nx * rows).transpose(0, 2, 1, 3).reshape(nz * rows, nx * rows)
        mirror = mirror.T.reshape(nx, 4, thin, nz * rows).transpose(0, 2, 1, 3).reshape(nx, thin, feeds)
        got = exchange(jnp.concatenate([mirror, halves], 1), along_x)
        halves = got[:, thin:, : nz * rows].transpose(1, 0, 2).reshape(16, feeds).astype(f32)
        both = halves[:8] + halves[8:]
        mirror = got[:, :thin].reshape(nx, thin, 4, nz * rows).transpose(2, 1, 0, 3).reshape(rows, feeds)
        return both[4:], both[:4], mirror

    kept, held, mirror = lax.cond(is_cal, with_cal, without, None)
    gains, calibrated = rescale(place, cal, kept, swap_cores(kept), held, mine, mirror)
    gains_now = lax.dynamic_slice_in_dim(gains, tm * rows, rows, 1).reshape(1, 2, 2, rows)
    return (calibrated.transpose(1, 0, 2)[None], gains_now)


def solution(mesh):
    return jax.shard_map(
        on_device,
        mesh=mesh,
        in_specs=(P("chan", None, None, "tm"), P("chan", None), P(), P("chan", None, None, "tm")),
        out_specs=(P("chan", "tm", None, None), P("chan", None, None, "tm")),
        check_vma=False,
    )
```

```python
import functools, math
import numpy as np
import jax
import jax.numpy as jnp
from jax import lax
from jax.experimental import pallas as pl
from jax.experimental.pallas import tpu as pltpu
from jax.sharding import PartitionSpec as P

ITERS = 8
epsilon = 1e-06
smoothing = 0.75

def gram_kernel(scale, cal_hbm, samples_hbm, flags_hbm, out_ref, is_cal_ref, cal_ref, samples_ref, flags_ref, left,
                right, sems):
    feeds, width = samples_ref.shape[1:]
    block = out_ref.shape[0]
    step = pl.program_id(0)

    @pl.when(step == 0)
    def _():
        copies = [
            pltpu.make_async_copy(cal_hbm, cal_ref, sems.at[0]),
            pltpu.make_async_copy(flags_hbm, flags_ref, sems.at[1]),
            pltpu.make_async_copy(samples_hbm.at[0], samples_ref.at[0], sems.at[2]),
            pltpu.make_async_copy(samples_hbm.at[1], samples_ref.at[1], sems.at[3]),
        ]
        for copy in copies:
            copy.start()
        copies[0].wait()
        chan = lax.axis_index("chan")
        is_cal_ref[0] = (cal_ref[chan // 2] == chan).astype(jnp.int32)
        copies[1].wait()
        good = jnp.broadcast_to(flags_ref[...].astype(jnp.float32), (128, feeds)).T
        good = jnp.concatenate([good] * (width // 128), 1).astype(jnp.bfloat16)
        copies[2].wait()
        re = samples_ref[0] * good
        right[:, :width] = re
        left[:, width:] = -re
        copies[3].wait()
        im = samples_ref[1] * good
        right[:, width:] = im
        left[:, :width] = im

    rows = pl.ds(pl.multiple_of(step * block, block), block)
    nt = (((1,), (1,)), ((), ()))
    both = lax.dot_general(right[rows, :], right[...], nt, preferred_element_type=jnp.float32)
    both += lax.dot_general(left[rows, :], right[...], nt, preferred_element_type=jnp.float32)
    out_ref[...] = (both * scale).astype(jnp.bfloat16)


def gram(cal_channel, samples, flags, all_time):
    _, feeds, width = samples.shape
    blocks = 4
    bf16 = jnp.bfloat16
    anywhere = pl.BlockSpec(memory_space=pl.ANY)
    return pl.pallas_call(
        functools.partial(gram_kernel, 1.0 / all_time),
        grid=(blocks,),
        out_shape=(jax.ShapeDtypeStruct((feeds, feeds), bf16), jax.ShapeDtypeStruct((1,), jnp.int32)),
        in_specs=[anywhere] * 3,
        out_specs=(
            pl.BlockSpec((feeds // blocks, feeds), lambda i: (i, 0)),
            pl.BlockSpec(memory_space=pltpu.SMEM),
        ),
        scratch_shapes=[
            pltpu.SMEM(cal_channel.shape, jnp.int32),
            pltpu.VMEM(samples.shape, bf16),
            pltpu.VMEM(flags.shape, jnp.int32),
            pltpu.VMEM((feeds, 2 * width), bf16),
            pltpu.VMEM((feeds, 2 * width), bf16),
            pltpu.SemaphoreType.DMA((4,)),
        ],
        compiler_params=pltpu.CompilerParams(vmem_limit_bytes=56 << 20),
        name="gram",
    )(cal_channel, samples, flags)


def fold_kernel(parts_ref, out_ref):
    parts = parts_ref[...].astype(jnp.float32)
    out_ref[...] = ((parts[0] + parts[1]) + (parts[2] + parts[3])).astype(jnp.bfloat16)


def fold(parts):
    _, rows, feeds = parts.shape
    block = 64
    return pl.pallas_call(
        fold_kernel,
        grid=(rows // block,),
        out_shape=jax.ShapeDtypeStruct((rows, feeds), jnp.bfloat16),
        in_specs=[pl.BlockSpec((4, block, feeds), lambda i: (0, i, 0))],
        out_specs=pl.BlockSpec((block, feeds), lambda i: (i, 0)),
        compiler_params=pltpu.CompilerParams(vmem_limit_bytes=40 << 20),
        name="fold",
    )(parts)


def basis_rows(feeds):
    f = np.arange(feeds, dtype=np.float64)
    ang = 2 * np.pi * np.arange(1, 3)[:, None] * f / feeds
    return (np.concatenate([np.cos(ang), np.sin(ang)]) / math.sqrt(feeds)).astype(np.float32)

def split3(v):
    hi = v.astype(jnp.bfloat16)
    rest = v - hi.astype(jnp.float32)
    mid = rest.astype(jnp.bfloat16)
    lo = (rest - mid.astype(jnp.float32)).astype(jnp.bfloat16)
    return hi, mid, lo

def total(v):
    return jnp.sum(v, axis=1, keepdims=True)

def solve_kernel(place_ref, own_ref, basis_ref, solved_ref, mirror_ref, mat_t):
    feeds = own_ref.shape[0]
    rows = mirror_ref.shape[0]
    for i in range(feeds // 256):
        mat_t[:, 256 * i:256 * (i + 1)] = own_ref[256 * i:256 * (i + 1), :].T
    mirror_ref[...] = mat_t[pl.ds(pl.multiple_of(place_ref[0] * rows, rows), rows), :].astype(jnp.float32)

    def sweep(_, carry):
        qr, qi, _, _ = carry
        s4 = jnp.concatenate([qr + qi, qr - qi], 0)
        hi, mid, lo = split3(s4)
        left = jnp.concatenate([hi, mid, lo, jnp.zeros_like(hi)], 0)
        with_t = jnp.dot(left, mat_t[...], preferred_element_type=jnp.float32)
        with_m = jnp.dot(left, own_ref[...], preferred_element_type=jnp.float32)
        with_t = (with_t[0:4] + with_t[4:8]) + with_t[8:12]
        with_m = (with_m[0:4] + with_m[4:8]) + with_m[8:12]
        zr = 0.5 * (with_t[2:4] + with_m[0:2])
        zi = 0.5 * (with_t[0:2] - with_m[2:4])
        one_r, two_r = zr[0:1], zr[1:2]
        one_i, two_i = zi[0:1], zi[1:2]
        n1 = total(one_r * one_r + one_i * one_i)
        cr = total(one_r * two_r + one_i * two_i)
        ci = total(one_r * two_i - one_i * two_r)
        first = jnp.sqrt(epsilon + n1)
        cr = cr / first
        ci = ci / first
        rest_r = two_r - (one_r * cr - one_i * ci) / first
        rest_i = two_i - (one_r * ci + one_i * cr) / first
        second = jnp.sqrt(epsilon + total(rest_r * rest_r + rest_i * rest_i))
        qr = jnp.concatenate([one_r / first, rest_r / second], 0)
        qi = jnp.concatenate([one_i / first, rest_i / second], 0)
        return qr, qi, first, second

    one = jnp.ones((1, 1), jnp.float32)
    qr, qi, first, second = lax.fori_loop(0, ITERS, sweep, (basis_ref[0:2], basis_ref[2:4], one, one))
    weights = jnp.concatenate([jnp.sqrt(first * feeds), jnp.sqrt(second * feeds)], 0)
    solved_ref[...] = jnp.concatenate([qr * weights, qi * weights], 0)


def solve(place, own, rows):
    feeds = own.shape[1]
    vm = pl.BlockSpec(memory_space=pltpu.VMEM)
    return pl.pallas_call(
        solve_kernel,
        out_shape=(jax.ShapeDtypeStruct((4, feeds), jnp.float32), jax.ShapeDtypeStruct((rows, feeds), jnp.float32)),
        in_specs=[pl.BlockSpec(memory_space=pltpu.SMEM), vm, vm],
        out_specs=(vm, vm),
        scratch_shapes=[pltpu.VMEM((feeds, feeds), jnp.bfloat16)],
        compiler_params=pltpu.CompilerParams(vmem_limit_bytes=40 << 20),
        name="solve",
    )(place, own, jnp.asarray(basis_rows(feeds)))


def rescale_kernel(place_ref, cal_ref, kept_ref, swapped_ref, state_ref, mine_ref, mirror_ref,
                   gains_ref, out_ref, turned):
    feeds = mine_ref.shape[1]
    rows = mine_ref.shape[0]
    place = place_ref[0]
    is_cal = cal_ref[0] > 0
    solved = jnp.where(is_cal, kept_ref[...], swapped_ref[...])
    state = jnp.where(is_cal, swapped_ref[...], state_ref[...])
    gains = smoothing * state + (1.0 - smoothing) * solved
    shift = (feeds - place * rows) % feeds
    gains_ref[...] = pltpu.roll(gains, shift, 1)[:, :rows]
    power = jnp.sum(gains * gains, axis=0, keepdims=True)
    mean_power = total(power) / feeds
    scale = jnp.sqrt((mean_power + epsilon) / (power + mean_power + epsilon))
    turned[...] = jnp.broadcast_to(scale, (128, feeds)).T
    down = turned[pl.ds(pl.multiple_of(place * rows, rows), rows), :]
    down = jnp.concatenate([down] * (feeds // 128), 1)
    factor = 0.5 * (down * scale)
    mine = mine_ref[...]
    mirror = mirror_ref[...]
    out_ref[0] = ((mine + mirror) * factor).astype(jnp.bfloat16)
    out_ref[1] = ((mine - mirror) * factor).astype(jnp.bfloat16)


def rescale(place, cal, kept, swapped, state, mine, mirror):
    rows, feeds = mine.shape
    vm = pl.BlockSpec(memory_space=pltpu.VMEM)
    sm = pl.BlockSpec(memory_space=pltpu.SMEM)
    return pl.pallas_call(
        rescale_kernel,
        out_shape=(jax.ShapeDtypeStruct((4, rows), jnp.float32), jax.ShapeDtypeStruct((2, rows, feeds), jnp.bfloat16)),
        in_specs=[sm, sm] + [vm] * 5,
        out_specs=(vm, vm),
        scratch_shapes=[pltpu.VMEM((feeds, 128), jnp.float32)],
        compiler_params=pltpu.CompilerParams(vmem_limit_bytes=40 << 20),
        name="rescale",
    )(place, cal, kept, swapped, state, mine, mirror)


def groups(mesh_shape_x, mesh_shape_z):
    along_x = [[x * mesh_shape_z + z for x in range(mesh_shape_x)] for z in range(mesh_shape_z)]
    along_z = [[x * mesh_shape_z + z for z in range(mesh_shape_z)] for x in range(mesh_shape_x)]
    return along_x, along_z


def exchange(value, which):
    return lax.all_to_all(value, "tm", 0, 0, axis_index_groups=which)


def swap_cores(value):
    count = lax.axis_size("chan")
    return lax.ppermute(value, "chan", [(i, i ^ 1) for i in range(count)])


def on_device(samples, feed_flags, cal_channel, gain_state):
    feeds = samples.shape[2]
    tm_count = lax.axis_size("tm")
    nx = nz = 4
    along_x, along_z = groups(nx, nz)
    rows = feeds // tm_count
    tm = lax.axis_index("tm")
    f32, bf16 = jnp.float32, jnp.bfloat16
    place = tm.reshape(1).astype(jnp.int32)
    own_state = gain_state[0].reshape(4, rows)
    other_state = swap_cores(own_state)
    packed, cal = gram(cal_channel, samples[0], feed_flags, samples.shape[3] * tm_count)
    packed, cal, own_state, other_state = lax.optimization_barrier((packed, cal, own_state, other_state))
    is_cal = cal[0] > 0

    def with_cal():
        part = fold(exchange(packed.reshape(nx, nz * rows, feeds), along_x))
        mine = jnp.sum(exchange(part.reshape(nz, rows, feeds), along_z).astype(f32), axis=0)
        got = exchange(jnp.broadcast_to(mine.astype(bf16)[None], (nz, rows, feeds)), along_z)
        got = exchange(jnp.broadcast_to(got.reshape(1, nz * rows, feeds), (nx, nz * rows, feeds)), along_x)
        solved, mirror = solve(place, got.reshape(feeds, feeds), rows)
        return solved, jnp.zeros((4, feeds), f32), mine, mirror

    def without():
        states = jnp.concatenate([own_state, other_state], 0)
        high = states.astype(bf16)
        low = (states - high.astype(f32)).astype(bf16)
        halves = jnp.broadcast_to(jnp.concatenate([high, low], 0)[None], (nx, 16, rows))
        halves = exchange(halves, along_x).transpose(1, 0, 2).reshape(16, nx * rows)
        halves, late = lax.optimization_barrier((halves, packed))
        part = fold(exchange(late.reshape(nx, nz * rows, feeds), along_x)).reshape(nz, rows, feeds)
        halves = jnp.pad(halves, ((0, 0), (0, feeds - nx * rows)))
        part = jnp.concatenate([part, jnp.broadcast_to(halves[None], (nz, 16, feeds))], 1)
        got = exchange(part, along_z)
        mine = jnp.sum(got[:, :rows].astype(f32), axis=0)
        mirror = exchange(mine.astype(bf16).T.reshape(tm_count, rows, rows), None)
        mirror = mirror.transpose(1, 0, 2).reshape(rows, feeds).astype(f32)
        halves = got[:, rows:, : nx * rows].astype(f32).reshape(nz, 2, 8, nx, rows)
        states = (halves[:, 0] + halves[:, 1]).transpose(1, 2, 0, 3).reshape(8, feeds)
        return states[4:], states[:4], mine, mirror

    kept, held, mine, mirror = lax.cond(is_cal, with_cal, without)
    gains, calibrated = rescale(place, cal, kept, swap_cores(kept), held, mine, mirror)
    return (calibrated.transpose(1, 0, 2)[None], gains.reshape(1, 2, 2, rows))


def solution(mesh):
    return jax.shard_map(
        on_device,
        mesh=mesh,
        in_specs=(P("chan", None, None, "tm"), P("chan", None), P(), P("chan", None, None, "tm")),
        out_specs=(P("chan", "tm", None, None), P("chan", None, None, "tm")),
        check_vma=False,
    )
```

```python
import functools, math
import numpy as np
import jax
import jax.numpy as jnp
from jax import lax
from jax.experimental import pallas as pl
from jax.experimental.pallas import tpu as pltpu
from jax.sharding import PartitionSpec as P

ITERS = 8
FIRST = 16
epsilon = 1e-06
smoothing = 0.75

def gram_kernel(scale, cal_hbm, samples_hbm, flags_hbm, out_ref, is_cal_ref, cal_ref, samples_ref, flags_ref, left,
                right, sems):
    feeds, width = samples_ref.shape[1:]
    block = out_ref.shape[0]
    step = pl.program_id(0)

    @pl.when(step == 0)
    def _():
        copies = [
            pltpu.make_async_copy(cal_hbm, cal_ref, sems.at[0]),
            pltpu.make_async_copy(flags_hbm, flags_ref, sems.at[1]),
            pltpu.make_async_copy(samples_hbm.at[0], samples_ref.at[0], sems.at[2]),
            pltpu.make_async_copy(samples_hbm.at[1], samples_ref.at[1], sems.at[3]),
        ]
        for copy in copies:
            copy.start()
        copies[0].wait()
        chan = lax.axis_index("chan")
        is_cal_ref[0] = (cal_ref[chan // 2] == chan).astype(jnp.int32)
        copies[1].wait()
        good = jnp.broadcast_to(flags_ref[...].astype(jnp.float32), (128, feeds)).T
        good = jnp.concatenate([good] * (width // 128), 1)
        copies[2].wait()
        re = samples_ref[0].astype(jnp.float32) * good
        left[:, :width] = re.astype(jnp.bfloat16)
        copies[3].wait()
        im = samples_ref[1].astype(jnp.float32) * good
        left[:, width:] = im.astype(jnp.bfloat16)
        right[:, :width] = (re - im).astype(jnp.bfloat16)
        right[:, width:] = (re + im).astype(jnp.bfloat16)

    rows = pl.ds(pl.multiple_of(step * block, block), block)
    nt = (((1,), (1,)), ((), ()))
    both = lax.dot_general(left[rows, :], right[...], nt, preferred_element_type=jnp.float32)
    out_ref[...] = (both * scale).astype(jnp.bfloat16)


def gram(cal_channel, samples, flags, all_time):
    _, feeds, width = samples.shape
    blocks = 4
    bf16 = jnp.bfloat16
    anywhere = pl.BlockSpec(memory_space=pl.ANY)
    return pl.pallas_call(
        functools.partial(gram_kernel, 1.0 / all_time),
        grid=(blocks,),
        out_shape=(jax.ShapeDtypeStruct((feeds, feeds), bf16), jax.ShapeDtypeStruct((1,), jnp.int32)),
        in_specs=[anywhere] * 3,
        out_specs=(
            pl.BlockSpec((feeds // blocks, feeds), lambda i: (i, 0)),
            pl.BlockSpec(memory_space=pltpu.SMEM),
        ),
        scratch_shapes=[
            pltpu.SMEM(cal_channel.shape, jnp.int32),
            pltpu.VMEM(samples.shape, bf16),
            pltpu.VMEM(flags.shape, jnp.int32),
            pltpu.VMEM((feeds, 2 * width), bf16),
            pltpu.VMEM((feeds, 2 * width), bf16),
            pltpu.SemaphoreType.DMA((4,)),
        ],
        compiler_params=pltpu.CompilerParams(vmem_limit_bytes=56 << 20),
        name="gram",
    )(cal_channel, samples, flags)


def fold_kernel(*refs):
    *part_refs, out_ref = refs
    at = 0
    for ref in part_refs:
        rows = ref.shape[1]
        for first in range(0, rows, 16):
            parts = [ref[k, first:first + 16, :].astype(jnp.float32) for k in range(4)]
            total_rows = (parts[0] + parts[1]) + (parts[2] + parts[3])
            out_ref[at + first:at + first + 16, :] = total_rows.astype(jnp.bfloat16)
        at += rows


def fold(*pieces):
    feeds = pieces[0].shape[2]
    rows = sum(piece.shape[1] for piece in pieces)
    vm = pl.BlockSpec(memory_space=pltpu.VMEM)
    return pl.pallas_call(
        fold_kernel,
        out_shape=jax.ShapeDtypeStruct((rows, feeds), jnp.bfloat16),
        in_specs=[vm] * len(pieces),
        out_specs=vm,
        compiler_params=pltpu.CompilerParams(vmem_limit_bytes=40 << 20),
        name="fold",
    )(*pieces)


def basis_rows(feeds):
    f = np.arange(feeds, dtype=np.float64)
    ang = 2 * np.pi * np.arange(1, 3)[:, None] * f / feeds
    return (np.concatenate([np.cos(ang), np.sin(ang)]) / math.sqrt(feeds)).astype(np.float32)

def split3(v):
    hi = v.astype(jnp.bfloat16)
    rest = v - hi.astype(jnp.float32)
    mid = rest.astype(jnp.bfloat16)
    lo = (rest - mid.astype(jnp.float32)).astype(jnp.bfloat16)
    return hi, mid, lo

def total(v):
    return jnp.sum(v, axis=1, keepdims=True)

def solve_kernel(place_ref, own_ref, basis_ref, solved_ref, mirror_ref, mat_t):
    feeds = own_ref.shape[0]
    rows = mirror_ref.shape[0]
    for i in range(feeds // 256):
        mat_t[:, 256 * i:256 * (i + 1)] = own_ref[256 * i:256 * (i + 1), :].T
    mirror_ref[...] = mat_t[pl.ds(pl.multiple_of(place_ref[0] * rows, rows), rows), :].astype(jnp.float32)

    def sweep(_, carry):
        qr, qi, _, _ = carry
        s4 = jnp.concatenate([qr + qi, qr - qi], 0)
        hi, mid, lo = split3(s4)
        left = jnp.concatenate([hi, mid, lo, jnp.zeros_like(hi)], 0)
        with_t = jnp.dot(left, mat_t[...], preferred_element_type=jnp.float32)
        with_m = jnp.dot(left, own_ref[...], preferred_element_type=jnp.float32)
        with_t = (with_t[0:4] + with_t[4:8]) + with_t[8:12]
        with_m = (with_m[0:4] + with_m[4:8]) + with_m[8:12]
        zr = 0.5 * (with_t[2:4] + with_m[0:2])
        zi = 0.5 * (with_t[0:2] - with_m[2:4])
        one_r, two_r = zr[0:1], zr[1:2]
        one_i, two_i = zi[0:1], zi[1:2]
        n1 = total(one_r * one_r + one_i * one_i)
        cr = total(one_r * two_r + one_i * two_i)
        ci = total(one_r * two_i - one_i * two_r)
        square = epsilon + n1
        inverse = lax.rsqrt(square)
        first = square * inverse
        cr = cr / square
        ci = ci / square
        rest_r = two_r - (one_r * cr - one_i * ci)
        rest_i = two_i - (one_r * ci + one_i * cr)
        square_two = epsilon + total(rest_r * rest_r + rest_i * rest_i)
        inverse_two = lax.rsqrt(square_two)
        second = square_two * inverse_two
        qr = jnp.concatenate([one_r * inverse, rest_r * inverse_two], 0)
        qi = jnp.concatenate([one_i * inverse, rest_i * inverse_two], 0)
        return qr, qi, first, second

    one = jnp.ones((1, 1), jnp.float32)
    qr, qi, first, second = lax.fori_loop(0, ITERS, sweep, (basis_ref[0:2], basis_ref[2:4], one, one))
    weights = jnp.concatenate([jnp.sqrt(first * feeds), jnp.sqrt(second * feeds)], 0)
    solved_ref[...] = jnp.concatenate([qr * weights, qi * weights], 0)


def solve(place, own, rows):
    feeds = own.shape[1]
    vm = pl.BlockSpec(memory_space=pltpu.VMEM)
    return pl.pallas_call(
        solve_kernel,
        out_shape=(jax.ShapeDtypeStruct((4, feeds), jnp.float32), jax.ShapeDtypeStruct((rows, feeds), jnp.float32)),
        in_specs=[pl.BlockSpec(memory_space=pltpu.SMEM), vm, vm],
        out_specs=(vm, vm),
        scratch_shapes=[pltpu.VMEM((feeds, feeds), jnp.bfloat16)],
        compiler_params=pltpu.CompilerParams(vmem_limit_bytes=40 << 20),
        name="solve",
    )(place, own, jnp.asarray(basis_rows(feeds)))


def rescale_kernel(place_ref, cal_ref, kept_ref, swapped_ref, state_ref, mine_ref, mirror_ref,
                   gains_ref, out_ref):
    feeds = mine_ref.shape[1]
    rows = mine_ref.shape[0]
    place = place_ref[0]
    is_cal = cal_ref[0] > 0
    solved = jnp.where(is_cal, kept_ref[...], swapped_ref[...])
    state = jnp.where(is_cal, swapped_ref[...], state_ref[...])
    gains = smoothing * state + (1.0 - smoothing) * solved
    shift = (feeds - place * rows) % feeds
    gains_ref[...] = pltpu.roll(gains, shift, 1)[:, :rows]
    power = jnp.sum(gains * gains, axis=0, keepdims=True)
    mean_power = total(power) / feeds
    scale = jnp.sqrt((mean_power + epsilon) / (power + mean_power + epsilon))
    down = jnp.broadcast_to(pltpu.roll(scale, shift, 1)[:, :128], (128, 128)).T[:rows]
    down = jnp.concatenate([down] * (feeds // 128), 1)
    factor = 0.5 * (down * scale)
    mine = mine_ref[...]
    mirror = mirror_ref[...]
    out_ref[:, 0, :] = ((mine + mirror) * factor).astype(jnp.bfloat16)
    out_ref[:, 1, :] = ((mine - mirror) * factor).astype(jnp.bfloat16)


def rescale(place, cal, kept, swapped, state, mine, mirror):
    rows, feeds = mine.shape
    vm = pl.BlockSpec(memory_space=pltpu.VMEM)
    sm = pl.BlockSpec(memory_space=pltpu.SMEM)
    return pl.pallas_call(
        rescale_kernel,
        out_shape=(jax.ShapeDtypeStruct((4, rows), jnp.float32), jax.ShapeDtypeStruct((rows, 2, feeds), jnp.bfloat16)),
        in_specs=[sm, sm] + [vm] * 5,
        out_specs=(vm, vm),
        compiler_params=pltpu.CompilerParams(vmem_limit_bytes=40 << 20),
        name="rescale",
    )(place, cal, kept, swapped, state, mine, mirror)


def groups(mesh_shape_x, mesh_shape_z):
    along_x = [[x * mesh_shape_z + z for x in range(mesh_shape_x)] for z in range(mesh_shape_z)]
    along_z = [[x * mesh_shape_z + z for z in range(mesh_shape_z)] for x in range(mesh_shape_x)]
    return along_x, along_z


def exchange(value, which):
    return lax.all_to_all(value, "tm", 0, 0, axis_index_groups=which)


def swap_cores(value):
    count = lax.axis_size("chan")
    return lax.ppermute(value, "chan", [(i, i ^ 1) for i in range(count)])


def on_device(samples, feed_flags, cal_channel, gain_state):
    feeds = samples.shape[2]
    tm_count = lax.axis_size("tm")
    nx = nz = 4
    along_x, along_z = groups(nx, nz)
    rows = feeds // tm_count
    tm = lax.axis_index("tm")
    f32, bf16 = jnp.float32, jnp.bfloat16
    place = tm.reshape(1).astype(jnp.int32)
    own_state = gain_state[0].reshape(4, rows)
    other_state = swap_cores(own_state)
    packed, cal = gram(cal_channel, samples[0], feed_flags, samples.shape[3] * tm_count)
    packed, cal, own_state, other_state = lax.optimization_barrier((packed, cal, own_state, other_state))
    is_cal = cal[0] > 0

    def with_cal():
        part = fold(exchange(packed.reshape(nx, nz * rows, feeds), along_x))
        mine = jnp.sum(exchange(part.reshape(nz, rows, feeds), along_z).astype(f32), axis=0)
        got = exchange(jnp.broadcast_to(mine.astype(bf16)[None], (nz, rows, feeds)), along_z)
        got = exchange(jnp.broadcast_to(got.reshape(1, nz * rows, feeds), (nx, nz * rows, feeds)), along_x)
        solved, mirror = solve(place, got.reshape(feeds, feeds), rows)
        return solved, jnp.zeros((4, feeds), f32), mine, mirror

    def without():
        blocks = packed.reshape(nx, nz * rows, feeds)
        lead = exchange(blocks[:, :FIRST], along_x)
        lead, trail = lax.optimization_barrier((lead, blocks[:, FIRST:]))
        part = fold(lead, exchange(trail, along_x))
        mine = jnp.sum(exchange(part.reshape(nz, rows, feeds), along_z).astype(f32), axis=0)
        states = jnp.concatenate([own_state, other_state], 0)
        high = states.astype(bf16)
        low = (states - high.astype(f32)).astype(bf16)
        halves = jnp.broadcast_to(jnp.concatenate([high, low], 0)[None], (tm_count, 16, rows))
        mirror = mine.astype(bf16).T.reshape(tm_count, rows, rows)
        got = exchange(jnp.concatenate([mirror, halves], 1), None)
        got = got.transpose(1, 0, 2).reshape(rows + 16, feeds).astype(f32)
        mirror, halves = got[:rows], got[rows:]
        states = halves[:8] + halves[8:]
        return states[4:], states[:4], mine, mirror

    kept, held, mine, mirror = lax.cond(is_cal, with_cal, without)
    gains, calibrated = rescale(place, cal, kept, swap_cores(kept), held, mine, mirror)
    return (calibrated[None], gains.reshape(1, 2, 2, rows))


def solution(mesh):
    return jax.shard_map(
        on_device,
        mesh=mesh,
        in_specs=(P("chan", None, None, "tm"), P("chan", None), P(), P("chan", None, None, "tm")),
        out_specs=(P("chan", "tm", None, None), P("chan", None, None, "tm")),
        check_vma=False,
    )
```

```python
import functools, math
import numpy as np
import jax
import jax.numpy as jnp
from jax import lax
from jax.experimental import pallas as pl
from jax.experimental.pallas import tpu as pltpu
from jax.sharding import PartitionSpec as P

ITERS = 8
FIRST = 16
epsilon = 1e-06
smoothing = 0.75

def gram_kernel(scale, cal_hbm, samples_hbm, flags_hbm, out_ref, is_cal_ref, cal_ref, samples_ref, flags_ref, left,
                right, sems):
    feeds, width = samples_ref.shape[1:]
    block = out_ref.shape[0]
    step = pl.program_id(0)

    @pl.when(step == 0)
    def _():
        copies = [
            pltpu.make_async_copy(cal_hbm, cal_ref, sems.at[0]),
            pltpu.make_async_copy(flags_hbm, flags_ref, sems.at[1]),
            pltpu.make_async_copy(samples_hbm.at[0], samples_ref.at[0], sems.at[2]),
            pltpu.make_async_copy(samples_hbm.at[1], samples_ref.at[1], sems.at[3]),
        ]
        for copy in copies:
            copy.start()
        copies[0].wait()
        chan = lax.axis_index("chan")
        is_cal_ref[0] = (cal_ref[chan // 2] == chan).astype(jnp.int32)
        copies[1].wait()
        good = jnp.broadcast_to(flags_ref[...].astype(jnp.float32), (128, feeds)).T
        good = jnp.concatenate([good] * (width // 128), 1)
        copies[2].wait()
        re = samples_ref[0].astype(jnp.float32) * good
        left[:, :width] = re.astype(jnp.bfloat16)
        copies[3].wait()
        im = samples_ref[1].astype(jnp.float32) * good
        left[:, width:] = im.astype(jnp.bfloat16)
        right[:, :width] = (re - im).astype(jnp.bfloat16)
        right[:, width:] = (re + im).astype(jnp.bfloat16)

    rows = pl.ds(pl.multiple_of(step * block, block), block)
    nt = (((1,), (1,)), ((), ()))
    both = lax.dot_general(left[rows, :], right[...], nt, preferred_element_type=jnp.float32)
    out_ref[...] = (both * scale).astype(jnp.bfloat16)


def gram(cal_channel, samples, flags, all_time):
    _, feeds, width = samples.shape
    blocks = 4
    bf16 = jnp.bfloat16
    anywhere = pl.BlockSpec(memory_space=pl.ANY)
    return pl.pallas_call(
        functools.partial(gram_kernel, 0.5 / all_time),
        grid=(blocks,),
        out_shape=(jax.ShapeDtypeStruct((feeds, feeds), bf16), jax.ShapeDtypeStruct((1,), jnp.int32)),
        in_specs=[anywhere] * 3,
        out_specs=(
            pl.BlockSpec((feeds // blocks, feeds), lambda i: (i, 0)),
            pl.BlockSpec(memory_space=pltpu.SMEM),
        ),
        scratch_shapes=[
            pltpu.SMEM(cal_channel.shape, jnp.int32),
            pltpu.VMEM(samples.shape, bf16),
            pltpu.VMEM(flags.shape, jnp.int32),
            pltpu.VMEM((feeds, 2 * width), bf16),
            pltpu.VMEM((feeds, 2 * width), bf16),
            pltpu.SemaphoreType.DMA((4,)),
        ],
        compiler_params=pltpu.CompilerParams(vmem_limit_bytes=56 << 20),
        name="gram",
    )(cal_channel, samples, flags)


def fold_kernel(*refs):
    *part_refs, out_ref = refs
    at = 0
    for ref in part_refs:
        rows = ref.shape[1]
        for first in range(0, rows, 16):
            parts = [ref[k, first:first + 16, :].astype(jnp.float32) for k in range(4)]
            total_rows = (parts[0] + parts[1]) + (parts[2] + parts[3])
            out_ref[at + first:at + first + 16, :] = total_rows.astype(jnp.bfloat16)
        at += rows


def fold(*pieces):
    feeds = pieces[0].shape[2]
    rows = sum(piece.shape[1] for piece in pieces)
    vm = pl.BlockSpec(memory_space=pltpu.VMEM)
    return pl.pallas_call(
        fold_kernel,
        out_shape=jax.ShapeDtypeStruct((rows, feeds), jnp.bfloat16),
        in_specs=[vm] * len(pieces),
        out_specs=vm,
        compiler_params=pltpu.CompilerParams(vmem_limit_bytes=40 << 20),
        name="fold",
    )(*pieces)


def basis_rows(feeds):
    f = np.arange(feeds, dtype=np.float64)
    ang = 2 * np.pi * np.arange(1, 3)[:, None] * f / feeds
    return (np.concatenate([np.cos(ang), np.sin(ang)]) / math.sqrt(feeds)).astype(np.float32)

def split3(v):
    hi = v.astype(jnp.bfloat16)
    rest = v - hi.astype(jnp.float32)
    mid = rest.astype(jnp.bfloat16)
    lo = (rest - mid.astype(jnp.float32)).astype(jnp.bfloat16)
    return hi, mid, lo

def total(v):
    return jnp.sum(v, axis=1, keepdims=True)

def solve_kernel(place_ref, own_ref, basis_ref, solved_ref, mirror_ref, mat_t):
    feeds = own_ref.shape[0]
    rows = mirror_ref.shape[0]
    for i in range(feeds // 256):
        mat_t[:, 256 * i:256 * (i + 1)] = own_ref[256 * i:256 * (i + 1), :].T
    mirror_ref[...] = mat_t[pl.ds(pl.multiple_of(place_ref[0] * rows, rows), rows), :].astype(jnp.float32)

    def sweep(_, carry):
        qr, qi, _, _ = carry
        s4 = jnp.concatenate([qr + qi, qr - qi], 0)
        hi, mid, lo = split3(s4)
        left = jnp.concatenate([hi, mid, lo, jnp.zeros_like(hi)], 0)
        with_t = jnp.dot(left, mat_t[...], preferred_element_type=jnp.float32)
        with_m = jnp.dot(left, own_ref[...], preferred_element_type=jnp.float32)
        with_t = (with_t[0:4] + with_t[4:8]) + with_t[8:12]
        with_m = (with_m[0:4] + with_m[4:8]) + with_m[8:12]
        zr = with_t[2:4] + with_m[0:2]
        zi = with_t[0:2] - with_m[2:4]
        one_r, two_r = zr[0:1], zr[1:2]
        one_i, two_i = zi[0:1], zi[1:2]
        n1 = total(one_r * one_r + one_i * one_i)
        cr = total(one_r * two_r + one_i * two_i)
        ci = total(one_r * two_i - one_i * two_r)
        square = epsilon + n1
        inverse = lax.rsqrt(square)
        first = square * inverse
        cr = cr / square
        ci = ci / square
        rest_r = two_r - (one_r * cr - one_i * ci)
        rest_i = two_i - (one_r * ci + one_i * cr)
        square_two = epsilon + total(rest_r * rest_r + rest_i * rest_i)
        inverse_two = lax.rsqrt(square_two)
        second = square_two * inverse_two
        qr = jnp.concatenate([one_r * inverse, rest_r * inverse_two], 0)
        qi = jnp.concatenate([one_i * inverse, rest_i * inverse_two], 0)
        return qr, qi, first, second

    one = jnp.ones((1, 1), jnp.float32)
    qr, qi, first, second = lax.fori_loop(0, ITERS, sweep, (basis_ref[0:2], basis_ref[2:4], one, one))
    weights = jnp.concatenate([jnp.sqrt(first * feeds), jnp.sqrt(second * feeds)], 0)
    solved_ref[...] = jnp.concatenate([qr * weights, qi * weights], 0)


def solve(place, own, rows):
    feeds = own.shape[1]
    vm = pl.BlockSpec(memory_space=pltpu.VMEM)
    return pl.pallas_call(
        solve_kernel,
        out_shape=(jax.ShapeDtypeStruct((4, feeds), jnp.float32), jax.ShapeDtypeStruct((rows, feeds), jnp.float32)),
        in_specs=[pl.BlockSpec(memory_space=pltpu.SMEM), vm, vm],
        out_specs=(vm, vm),
        scratch_shapes=[pltpu.VMEM((feeds, feeds), jnp.bfloat16)],
        compiler_params=pltpu.CompilerParams(vmem_limit_bytes=40 << 20),
        name="solve",
    )(place, own, jnp.asarray(basis_rows(feeds)))


def rescale_kernel(place_ref, cal_ref, kept_ref, swapped_ref, state_ref, mine_ref, mirror_ref,
                   gains_ref, out_ref):
    feeds = mine_ref.shape[1]
    rows = mine_ref.shape[0]
    place = place_ref[0]
    is_cal = cal_ref[0] > 0
    solved = jnp.where(is_cal, kept_ref[...], swapped_ref[...])
    state = jnp.where(is_cal, swapped_ref[...], state_ref[...])
    gains = smoothing * state + (1.0 - smoothing) * solved
    shift = (feeds - place * rows) % feeds
    gains_ref[...] = pltpu.roll(gains, shift, 1)[:, :rows]
    power = jnp.sum(gains * gains, axis=0, keepdims=True)
    mean_power = total(power) / feeds
    scale = jnp.sqrt((mean_power + epsilon) / (power + mean_power + epsilon))
    down = jnp.broadcast_to(pltpu.roll(scale, shift, 1)[:, :128], (128, 128)).T[:rows]
    down = jnp.concatenate([down] * (feeds // 128), 1)
    factor = down * scale
    mine = mine_ref[...]
    mirror = mirror_ref[...]
    out_ref[:, 0, :] = ((mine + mirror) * factor).astype(jnp.bfloat16)
    out_ref[:, 1, :] = ((mine - mirror) * factor).astype(jnp.bfloat16)


def rescale(place, cal, kept, swapped, state, mine, mirror):
    rows, feeds = mine.shape
    vm = pl.BlockSpec(memory_space=pltpu.VMEM)
    sm = pl.BlockSpec(memory_space=pltpu.SMEM)
    return pl.pallas_call(
        rescale_kernel,
        out_shape=(jax.ShapeDtypeStruct((4, rows), jnp.float32), jax.ShapeDtypeStruct((rows, 2, feeds), jnp.bfloat16)),
        in_specs=[sm, sm] + [vm] * 5,
        out_specs=(vm, vm),
        compiler_params=pltpu.CompilerParams(vmem_limit_bytes=40 << 20),
        name="rescale",
    )(place, cal, kept, swapped, state, mine, mirror)


def groups(mesh_shape_x, mesh_shape_z):
    along_x = [[x * mesh_shape_z + z for x in range(mesh_shape_x)] for z in range(mesh_shape_z)]
    along_z = [[x * mesh_shape_z + z for z in range(mesh_shape_z)] for x in range(mesh_shape_x)]
    return along_x, along_z


def exchange(value, which):
    return lax.all_to_all(value, "tm", 0, 0, axis_index_groups=which)


def swap_cores(value):
    count = lax.axis_size("chan")
    return lax.ppermute(value, "chan", [(i, i ^ 1) for i in range(count)])


def on_device(samples, feed_flags, cal_channel, gain_state):
    feeds = samples.shape[2]
    tm_count = lax.axis_size("tm")
    nx = nz = 4
    along_x, along_z = groups(nx, nz)
    rows = feeds // tm_count
    tm = lax.axis_index("tm")
    f32, bf16 = jnp.float32, jnp.bfloat16
    place = tm.reshape(1).astype(jnp.int32)
    own_state = gain_state[0].reshape(4, rows)
    other_state = swap_cores(own_state)
    packed, cal = gram(cal_channel, samples[0], feed_flags, samples.shape[3] * tm_count)
    packed, cal, own_state, other_state = lax.optimization_barrier((packed, cal, own_state, other_state))
    is_cal = cal[0] > 0
    odd = lax.axis_index("chan") % 2 == 1

    def with_cal():
        part = fold(exchange(packed.reshape(nx, nz * rows, feeds), along_x))
        mine = jnp.sum(exchange(part.reshape(nz, rows, feeds), along_z).astype(f32), axis=0)
        got = exchange(jnp.broadcast_to(mine.astype(bf16)[None], (nz, rows, feeds)), along_z)
        got = exchange(jnp.broadcast_to(got.reshape(1, nz * rows, feeds), (nx, nz * rows, feeds)), along_x)
        solved, mirror = solve(place, got.reshape(feeds, feeds), rows)
        return solved, jnp.zeros((4, feeds), f32), mine, mirror

    def around_x(value):
        here = tm // nz
        got = [lax.dynamic_index_in_dim(value, here, 0, keepdims=False)]
        for shift in range(1, nx):
            pairs = [(i, (i + shift * nz) % tm_count) for i in range(tm_count)]
            block = lax.dynamic_index_in_dim(value, (here + shift) % nx, 0, keepdims=False)
            got.append(lax.ppermute(block, "tm", pairs))
        return jnp.stack(got)

    def without():
        blocks = packed.reshape(nx, nz * rows, feeds)
        lead = lax.cond(odd, around_x, lambda value: exchange(value, along_x), blocks[:, :FIRST])
        lead, trail = lax.optimization_barrier((lead, blocks[:, FIRST:]))
        part = fold(lead, exchange(trail, along_x))
        mine = jnp.sum(exchange(part.reshape(nz, rows, feeds), along_z).astype(f32), axis=0)
        states = jnp.concatenate([own_state, other_state], 0)
        high = states.astype(bf16)
        low = (states - high.astype(f32)).astype(bf16)
        halves = jnp.broadcast_to(jnp.concatenate([high, low], 0)[None], (tm_count, 16, rows))
        mirror = mine.astype(bf16).T.reshape(tm_count, rows, rows)
        got = exchange(jnp.concatenate([mirror, halves], 1), None)
        got = got.transpose(1, 0, 2).reshape(rows + 16, feeds).astype(f32)
        mirror, halves = got[:rows], got[rows:]
        states = halves[:8] + halves[8:]
        return states[4:], states[:4], mine, mirror

    kept, held, mine, mirror = lax.cond(is_cal, with_cal, without)
    gains, calibrated = rescale(place, cal, kept, swap_cores(kept), held, mine, mirror)
    return (calibrated[None], gains.reshape(1, 2, 2, rows))


def solution(mesh):
    return jax.shard_map(
        on_device,
        mesh=mesh,
        in_specs=(P("chan", None, None, "tm"), P("chan", None), P(), P("chan", None, None, "tm")),
        out_specs=(P("chan", "tm", None, None), P("chan", None, None, "tm")),
        check_vma=False,
    )
```

```python
import functools, math
import numpy as np
import jax
import jax.numpy as jnp
from jax import lax
from jax.experimental import pallas as pl
from jax.experimental.pallas import tpu as pltpu
from jax.sharding import PartitionSpec as P

ITERS = 8
FIRST = 16
SHIFTS = (2, 1, 3)
epsilon = 1e-06
smoothing = 0.75

def gram_kernel(scale, cal_hbm, samples_hbm, flags_hbm, out_ref, is_cal_ref, cal_ref, samples_ref, flags_ref, left,
                right, sems):
    feeds, width = samples_ref.shape[1:]
    block = out_ref.shape[0]
    step = pl.program_id(0)

    @pl.when(step == 0)
    def _():
        copies = [
            pltpu.make_async_copy(cal_hbm, cal_ref, sems.at[0]),
            pltpu.make_async_copy(flags_hbm, flags_ref, sems.at[1]),
            pltpu.make_async_copy(samples_hbm.at[0], samples_ref.at[0], sems.at[2]),
            pltpu.make_async_copy(samples_hbm.at[1], samples_ref.at[1], sems.at[3]),
        ]
        for copy in copies:
            copy.start()
        copies[0].wait()
        chan = lax.axis_index("chan")
        is_cal_ref[0] = (cal_ref[chan // 2] == chan).astype(jnp.int32)
        copies[1].wait()
        good = jnp.broadcast_to(flags_ref[...].astype(jnp.float32), (128, feeds)).T
        good = jnp.concatenate([good] * (width // 128), 1)
        copies[2].wait()
        re = samples_ref[0].astype(jnp.float32) * good
        left[:, :width] = re.astype(jnp.bfloat16)
        copies[3].wait()
        im = samples_ref[1].astype(jnp.float32) * good
        left[:, width:] = im.astype(jnp.bfloat16)
        right[:, :width] = (re - im).astype(jnp.bfloat16)
        right[:, width:] = (re + im).astype(jnp.bfloat16)

    rows = pl.ds(pl.multiple_of(step * block, block), block)
    nt = (((1,), (1,)), ((), ()))
    both = lax.dot_general(left[rows, :], right[...], nt, preferred_element_type=jnp.float32)
    out_ref[...] = (both * scale).astype(jnp.bfloat16)


def gram(cal_channel, samples, flags, all_time):
    _, feeds, width = samples.shape
    blocks = 4
    bf16 = jnp.bfloat16
    anywhere = pl.BlockSpec(memory_space=pl.ANY)
    return pl.pallas_call(
        functools.partial(gram_kernel, 0.5 / all_time),
        grid=(blocks,),
        out_shape=(jax.ShapeDtypeStruct((feeds, feeds), bf16), jax.ShapeDtypeStruct((1,), jnp.int32)),
        in_specs=[anywhere] * 3,
        out_specs=(
            pl.BlockSpec((feeds // blocks, feeds), lambda i: (i, 0)),
            pl.BlockSpec(memory_space=pltpu.SMEM),
        ),
        scratch_shapes=[
            pltpu.SMEM(cal_channel.shape, jnp.int32),
            pltpu.VMEM(samples.shape, bf16),
            pltpu.VMEM(flags.shape, jnp.int32),
            pltpu.VMEM((feeds, 2 * width), bf16),
            pltpu.VMEM((feeds, 2 * width), bf16),
            pltpu.SemaphoreType.DMA((4,)),
        ],
        compiler_params=pltpu.CompilerParams(vmem_limit_bytes=56 << 20),
        name="gram",
    )(cal_channel, samples, flags)


def fold_kernel(count, *refs):
    part_refs, out_refs = refs[:count], refs[count:]
    at = 0
    for ref in part_refs:
        rows = ref.shape[1]
        for first in range(0, rows, 16):
            parts = [ref[k, first:first + 16, :].astype(jnp.float32) for k in range(4)]
            total_rows = (parts[0] + parts[1]) + (parts[2] + parts[3])
            for out_ref in out_refs:
                out_ref[at + first:at + first + 16, :] = total_rows.astype(jnp.bfloat16)
        at += rows


def fold(*pieces, copies=1):
    feeds = pieces[0].shape[2]
    rows = sum(piece.shape[1] for piece in pieces)
    vm = pl.BlockSpec(memory_space=pltpu.VMEM)
    out = jax.ShapeDtypeStruct((rows, feeds), jnp.bfloat16)
    out = pl.pallas_call(
        functools.partial(fold_kernel, len(pieces)),
        out_shape=[out] * copies,
        in_specs=[vm] * len(pieces),
        out_specs=[vm] * copies,
        compiler_params=pltpu.CompilerParams(vmem_limit_bytes=40 << 20),
        name="fold",
    )(*pieces)
    return out[0] if copies == 1 else out


def basis_rows(feeds):
    f = np.arange(feeds, dtype=np.float64)
    ang = 2 * np.pi * np.arange(1, 3)[:, None] * f / feeds
    return (np.concatenate([np.cos(ang), np.sin(ang)]) / math.sqrt(feeds)).astype(np.float32)

def split3(v):
    hi = v.astype(jnp.bfloat16)
    rest = v - hi.astype(jnp.float32)
    mid = rest.astype(jnp.bfloat16)
    lo = (rest - mid.astype(jnp.float32)).astype(jnp.bfloat16)
    return hi, mid, lo

def total(v):
    return jnp.sum(v, axis=1, keepdims=True)

def solve_kernel(place_ref, *refs):
    *slab_refs, basis_ref, solved_ref, mirror_ref, own_ref, mat_t = refs
    feeds = own_ref.shape[0]
    rows = mirror_ref.shape[0]
    size = slab_refs[0].shape[0]
    here = place_ref[0] * rows // size
    for shift, ref in zip((0,) + SHIFTS, slab_refs):
        first = (here + len(slab_refs) - shift) % len(slab_refs)
        own_ref[pl.ds(pl.multiple_of(first * size, size), size), :] = ref[...]
    for i in range(feeds // size):
        mat_t[:, size * i:size * (i + 1)] = own_ref[size * i:size * (i + 1), :].T
    mirror_ref[...] = mat_t[pl.ds(pl.multiple_of(place_ref[0] * rows, rows), rows), :]

    def sweep(_, carry):
        qr, qi, _, _ = carry
        s4 = jnp.concatenate([qr + qi, qr - qi], 0)
        hi, mid, lo = split3(s4)
        left = jnp.concatenate([hi, mid, lo, jnp.zeros_like(hi)], 0)
        with_t = jnp.dot(left, mat_t[...], preferred_element_type=jnp.float32)
        with_m = jnp.dot(left, own_ref[...], preferred_element_type=jnp.float32)
        with_t = (with_t[0:4] + with_t[4:8]) + with_t[8:12]
        with_m = (with_m[0:4] + with_m[4:8]) + with_m[8:12]
        zr = with_t[2:4] + with_m[0:2]
        zi = with_t[0:2] - with_m[2:4]
        one_r, two_r = zr[0:1], zr[1:2]
        one_i, two_i = zi[0:1], zi[1:2]
        n1 = total(one_r * one_r + one_i * one_i)
        cr = total(one_r * two_r + one_i * two_i)
        ci = total(one_r * two_i - one_i * two_r)
        square = epsilon + n1
        inverse = lax.rsqrt(square)
        first = square * inverse
        cr = cr / square
        ci = ci / square
        rest_r = two_r - (one_r * cr - one_i * ci)
        rest_i = two_i - (one_r * ci + one_i * cr)
        square_two = epsilon + total(rest_r * rest_r + rest_i * rest_i)
        inverse_two = lax.rsqrt(square_two)
        second = square_two * inverse_two
        qr = jnp.concatenate([one_r * inverse, rest_r * inverse_two], 0)
        qi = jnp.concatenate([one_i * inverse, rest_i * inverse_two], 0)
        return qr, qi, first, second

    one = jnp.ones((1, 1), jnp.float32)
    qr, qi, first, second = lax.fori_loop(0, ITERS, sweep, (basis_ref[0:2], basis_ref[2:4], one, one))
    weights = jnp.concatenate([jnp.sqrt(first * feeds), jnp.sqrt(second * feeds)], 0)
    solved_ref[...] = jnp.concatenate([qr * weights, qi * weights], 0)


def solve(place, slabs, rows):
    feeds = slabs[0].shape[1]
    vm = pl.BlockSpec(memory_space=pltpu.VMEM)
    return pl.pallas_call(
        solve_kernel,
        out_shape=(jax.ShapeDtypeStruct((4, feeds), jnp.float32), jax.ShapeDtypeStruct((rows, feeds), jnp.bfloat16)),
        in_specs=[pl.BlockSpec(memory_space=pltpu.SMEM)] + [vm] * (len(slabs) + 1),
        out_specs=(vm, vm),
        scratch_shapes=[pltpu.VMEM((feeds, feeds), jnp.bfloat16)] * 2,
        compiler_params=pltpu.CompilerParams(vmem_limit_bytes=40 << 20),
        name="solve",
    )(place, *slabs, jnp.asarray(basis_rows(feeds)))


def rescale_kernel(place_ref, cal_ref, kept_ref, swapped_ref, state_ref, mine_hbm, mirror_hbm,
                   gains_ref, out_ref, mine_ref, mirror_ref, sems):
    rows, feeds = mine_ref.shape
    place = place_ref[0]
    is_cal = cal_ref[0] > 0
    copies = [
        pltpu.make_async_copy(mine_hbm, mine_ref, sems.at[0]),
        pltpu.make_async_copy(mirror_hbm, mirror_ref, sems.at[1]),
    ]
    for copy in copies:
        copy.start()
    solved = jnp.where(is_cal, kept_ref[...], swapped_ref[...])
    state = jnp.where(is_cal, swapped_ref[...], state_ref[...])
    gains = smoothing * state + (1.0 - smoothing) * solved
    shift = (feeds - place * rows) % feeds
    gains_ref[...] = pltpu.roll(gains, shift, 1)[:, :rows]
    power = jnp.sum(gains * gains, axis=0, keepdims=True)
    mean_power = total(power) / feeds
    scale = jnp.sqrt((mean_power + epsilon) / (power + mean_power + epsilon))
    down = jnp.broadcast_to(pltpu.roll(scale, shift, 1)[:, :128], (128, 128)).T[:rows]
    down = jnp.concatenate([down] * (feeds // 128), 1)
    factor = down * scale
    for copy in copies:
        copy.wait()
    mine = mine_ref[...].astype(jnp.float32)
    mirror = mirror_ref[...].astype(jnp.float32)
    out_ref[:, 0, :] = ((mine + mirror) * factor).astype(jnp.bfloat16)
    out_ref[:, 1, :] = ((mine - mirror) * factor).astype(jnp.bfloat16)


def rescale(place, cal, kept, swapped, state, mine, mirror):
    rows, feeds = mine.shape
    vm = pl.BlockSpec(memory_space=pltpu.VMEM)
    sm = pl.BlockSpec(memory_space=pltpu.SMEM)
    return pl.pallas_call(
        rescale_kernel,
        out_shape=(jax.ShapeDtypeStruct((4, rows), jnp.float32), jax.ShapeDtypeStruct((rows, 2, feeds), jnp.bfloat16)),
        in_specs=[sm, sm] + [vm] * 3 + [pl.BlockSpec(memory_space=pl.ANY)] * 2,
        out_specs=(vm, vm),
        scratch_shapes=[pltpu.VMEM((rows, feeds), jnp.bfloat16)] * 2 + [pltpu.SemaphoreType.DMA((2,))],
        compiler_params=pltpu.CompilerParams(vmem_limit_bytes=40 << 20),
        name="rescale",
    )(place, cal, kept, swapped, state, mine, mirror)


def groups(mesh_shape_x, mesh_shape_z):
    along_x = [[x * mesh_shape_z + z for x in range(mesh_shape_x)] for z in range(mesh_shape_z)]
    along_z = [[x * mesh_shape_z + z for z in range(mesh_shape_z)] for x in range(mesh_shape_x)]
    return along_x, along_z


def exchange(value, which):
    return lax.all_to_all(value, "tm", 0, 0, axis_index_groups=which)


def swap_cores(value):
    count = lax.axis_size("chan")
    return lax.ppermute(value, "chan", [(i, i ^ 1) for i in range(count)])


def on_device(samples, feed_flags, cal_channel, gain_state):
    feeds = samples.shape[2]
    tm_count = lax.axis_size("tm")
    nx = nz = 4
    along_x, along_z = groups(nx, nz)
    rows = feeds // tm_count
    tm = lax.axis_index("tm")
    f32, bf16 = jnp.float32, jnp.bfloat16
    place = tm.reshape(1).astype(jnp.int32)
    own_state = gain_state[0].reshape(4, rows)
    other_state = swap_cores(own_state)
    packed, cal = gram(cal_channel, samples[0], feed_flags, samples.shape[3] * tm_count)
    packed, cal, own_state, other_state = lax.optimization_barrier((packed, cal, own_state, other_state))
    is_cal = cal[0] > 0
    odd = lax.axis_index("chan") % 2 == 1

    def shifted_x(block, shift):
        return lax.ppermute(block, "tm", [(i, (i + shift * nz) % tm_count) for i in range(tm_count)])

    def with_cal():
        part = fold(exchange(packed.reshape(nx, nz * rows, feeds), along_x))
        sent, mine = fold(exchange(part.reshape(nz, rows, feeds), along_z), copies=2)
        got = exchange(jnp.broadcast_to(sent[None], (nz, rows, feeds)), along_z)
        slab = got.reshape(nz * rows, feeds)
        slabs = [shifted_x(slab, shift) for shift in SHIFTS]
        solved, mirror = solve(place, [slab] + slabs, rows)
        return solved, jnp.zeros((4, feeds), f32), mine, mirror

    def around_x(value):
        here = tm // nz
        got = [lax.dynamic_index_in_dim(value, here, 0, keepdims=False)]
        for shift in range(1, nx):
            got.append(shifted_x(lax.dynamic_index_in_dim(value, (here + shift) % nx, 0, keepdims=False), shift))
        return jnp.stack(got)

    def without():
        blocks = packed.reshape(nx, nz * rows, feeds)
        lead = lax.cond(odd, around_x, lambda value: exchange(value, along_x), blocks[:, :FIRST])
        lead, trail = lax.optimization_barrier((lead, blocks[:, FIRST:]))
        part = fold(lead, exchange(trail, along_x))
        mine = fold(exchange(part.reshape(nz, rows, feeds), along_z))
        states = jnp.concatenate([own_state, other_state], 0)
        high = states.astype(bf16)
        low = (states - high.astype(f32)).astype(bf16)
        halves = jnp.broadcast_to(jnp.concatenate([high, low], 0)[None], (tm_count, 16, rows))
        mirror = mine.T.reshape(tm_count, rows, rows)
        got = exchange(jnp.concatenate([mirror, halves], 1), None)
        got = got.transpose(1, 0, 2).reshape(rows + 16, feeds)
        mirror, halves = got[:rows], got[rows:].astype(f32)
        states = halves[:8] + halves[8:]
        return states[4:], states[:4], mine, mirror

    kept, held, mine, mirror = lax.cond(is_cal, with_cal, without)
    gains, calibrated = rescale(place, cal, kept, swap_cores(kept), held, mine, mirror)
    return (calibrated[None], gains.reshape(1, 2, 2, rows))


def solution(mesh):
    return jax.shard_map(
        on_device,
        mesh=mesh,
        in_specs=(P("chan", None, None, "tm"), P("chan", None), P(), P("chan", None, None, "tm")),
        out_specs=(P("chan", "tm", None, None), P("chan", None, None, "tm")),
        check_vma=False,
    )
```

```python
import functools, math
import numpy as np
import jax
import jax.numpy as jnp
from jax import lax
from jax.experimental import pallas as pl
from jax.experimental.pallas import tpu as pltpu
from jax.sharding import PartitionSpec as P

ITERS = 8
FIRST = 16
epsilon = 1e-06
smoothing = 0.75

def gram_kernel(scale, cal_hbm, samples_hbm, flags_hbm, out_ref, is_cal_ref, cal_ref, samples_ref, flags_ref, left,
                right, sems):
    feeds, width = samples_ref.shape[1:]
    block = feeds // 4
    copies = [
        pltpu.make_async_copy(cal_hbm, cal_ref, sems.at[0]),
        pltpu.make_async_copy(flags_hbm, flags_ref, sems.at[1]),
        pltpu.make_async_copy(samples_hbm.at[0], samples_ref.at[0], sems.at[2]),
        pltpu.make_async_copy(samples_hbm.at[1], samples_ref.at[1], sems.at[3]),
    ]
    for copy in copies:
        copy.start()
    copies[0].wait()
    chan = lax.axis_index("chan")
    is_cal_ref[0] = (cal_ref[chan // 2] == chan).astype(jnp.int32)
    copies[1].wait()
    good = jnp.broadcast_to(flags_ref[...].astype(jnp.float32), (128, feeds)).T
    good = jnp.concatenate([good] * (width // 128), 1)
    copies[2].wait()
    re = samples_ref[0].astype(jnp.float32) * good
    left[:, :width] = re.astype(jnp.bfloat16)
    copies[3].wait()
    im = samples_ref[1].astype(jnp.float32) * good
    left[:, width:] = im.astype(jnp.bfloat16)
    right[:, :width] = (re - im).astype(jnp.bfloat16)
    right[:, width:] = (re + im).astype(jnp.bfloat16)

    def rows_of(step, _):
        rows = pl.ds(pl.multiple_of(step * block, block), block)
        nt = (((1,), (1,)), ((), ()))
        both = lax.dot_general(left[rows, :], right[...], nt, preferred_element_type=jnp.float32)
        out_ref[rows, :] = (both * scale).astype(jnp.bfloat16)
        return 0

    lax.fori_loop(0, 4, rows_of, 0)


def gram(cal_channel, samples, flags, all_time):
    _, feeds, width = samples.shape
    bf16 = jnp.bfloat16
    outside = pl.BlockSpec(memory_space=pltpu.HBM)
    return pl.pallas_call(
        functools.partial(gram_kernel, 0.5 / all_time),
        out_shape=(jax.ShapeDtypeStruct((feeds, feeds), bf16), jax.ShapeDtypeStruct((1,), jnp.int32)),
        in_specs=[outside] * 3,
        out_specs=(pl.BlockSpec(memory_space=pltpu.VMEM), pl.BlockSpec(memory_space=pltpu.SMEM)),
        scratch_shapes=[
            pltpu.SMEM(cal_channel.shape, jnp.int32),
            pltpu.VMEM(samples.shape, bf16),
            pltpu.VMEM(flags.shape, jnp.int32),
            pltpu.VMEM((feeds, 2 * width), bf16),
            pltpu.VMEM((feeds, 2 * width), bf16),
            pltpu.SemaphoreType.DMA((4,)),
        ],
        compiler_params=pltpu.CompilerParams(vmem_limit_bytes=56 << 20),
        name="gram",
    )(cal_channel, samples, flags)


def fold_kernel(*refs):
    *part_refs, out_ref = refs
    at = 0
    for ref in part_refs:
        rows = ref.shape[1]
        for first in range(0, rows, 16):
            parts = [ref[k, first:first + 16, :].astype(jnp.float32) for k in range(4)]
            total_rows = (parts[0] + parts[1]) + (parts[2] + parts[3])
            out_ref[at + first:at + first + 16, :] = total_rows.astype(jnp.bfloat16)
        at += rows


def fold(*pieces):
    feeds = pieces[0].shape[2]
    rows = sum(piece.shape[1] for piece in pieces)
    vm = pl.BlockSpec(memory_space=pltpu.VMEM)
    return pl.pallas_call(
        fold_kernel,
        out_shape=jax.ShapeDtypeStruct((rows, feeds), jnp.bfloat16),
        in_specs=[vm] * len(pieces),
        out_specs=vm,
        compiler_params=pltpu.CompilerParams(vmem_limit_bytes=40 << 20),
        name="fold",
    )(*pieces)


def basis_rows(feeds):
    f = np.arange(feeds, dtype=np.float64)
    ang = 2 * np.pi * np.arange(1, 3)[:, None] * f / feeds
    return (np.concatenate([np.cos(ang), np.sin(ang)]) / math.sqrt(feeds)).astype(np.float32)

def split3(v):
    hi = v.astype(jnp.bfloat16)
    rest = v - hi.astype(jnp.float32)
    mid = rest.astype(jnp.bfloat16)
    lo = (rest - mid.astype(jnp.float32)).astype(jnp.bfloat16)
    return hi, mid, lo

def total(v):
    return jnp.sum(v, axis=1, keepdims=True)

def solve_kernel(place_ref, own_ref, basis_ref, solved_ref, mirror_ref, mat_t):
    feeds = own_ref.shape[0]
    rows = mirror_ref.shape[0]
    for i in range(feeds // 256):
        mat_t[:, 256 * i:256 * (i + 1)] = own_ref[256 * i:256 * (i + 1), :].T
    mirror_ref[...] = mat_t[pl.ds(pl.multiple_of(place_ref[0] * rows, rows), rows), :].astype(jnp.float32)

    def sweep(_, carry):
        qr, qi, _, _ = carry
        s4 = jnp.concatenate([qr + qi, qr - qi], 0)
        hi, mid, lo = split3(s4)
        left = jnp.concatenate([hi, mid, lo, jnp.zeros_like(hi)], 0)
        with_t = jnp.dot(left, mat_t[...], preferred_element_type=jnp.float32)
        with_m = jnp.dot(left, own_ref[...], preferred_element_type=jnp.float32)
        with_t = (with_t[0:4] + with_t[4:8]) + with_t[8:12]
        with_m = (with_m[0:4] + with_m[4:8]) + with_m[8:12]
        zr = with_t[2:4] + with_m[0:2]
        zi = with_t[0:2] - with_m[2:4]
        one_r, two_r = zr[0:1], zr[1:2]
        one_i, two_i = zi[0:1], zi[1:2]
        n1 = total(one_r * one_r + one_i * one_i)
        cr = total(one_r * two_r + one_i * two_i)
        ci = total(one_r * two_i - one_i * two_r)
        square = epsilon + n1
        inverse = lax.rsqrt(square)
        first = square * inverse
        cr = cr / square
        ci = ci / square
        rest_r = two_r - (one_r * cr - one_i * ci)
        rest_i = two_i - (one_r * ci + one_i * cr)
        square_two = epsilon + total(rest_r * rest_r + rest_i * rest_i)
        inverse_two = lax.rsqrt(square_two)
        second = square_two * inverse_two
        qr = jnp.concatenate([one_r * inverse, rest_r * inverse_two], 0)
        qi = jnp.concatenate([one_i * inverse, rest_i * inverse_two], 0)
        return qr, qi, first, second

    one = jnp.ones((1, 1), jnp.float32)
    qr, qi, first, second = lax.fori_loop(0, ITERS, sweep, (basis_ref[0:2], basis_ref[2:4], one, one))
    weights = jnp.concatenate([jnp.sqrt(first * feeds), jnp.sqrt(second * feeds)], 0)
    solved_ref[...] = jnp.concatenate([qr * weights, qi * weights], 0)


def solve(place, own, rows):
    feeds = own.shape[1]
    vm = pl.BlockSpec(memory_space=pltpu.VMEM)
    return pl.pallas_call(
        solve_kernel,
        out_shape=(jax.ShapeDtypeStruct((4, feeds), jnp.float32), jax.ShapeDtypeStruct((rows, feeds), jnp.float32)),
        in_specs=[pl.BlockSpec(memory_space=pltpu.SMEM), vm, vm],
        out_specs=(vm, vm),
        scratch_shapes=[pltpu.VMEM((feeds, feeds), jnp.bfloat16)],
        compiler_params=pltpu.CompilerParams(vmem_limit_bytes=40 << 20),
        name="solve",
    )(place, own, jnp.asarray(basis_rows(feeds)))


def rescale_kernel(place_ref, cal_ref, kept_ref, swapped_ref, state_ref, mine_ref, mirror_ref,
                   gains_ref, out_ref):
    feeds = mine_ref.shape[1]
    rows = mine_ref.shape[0]
    place = place_ref[0]
    is_cal = cal_ref[0] > 0
    solved = jnp.where(is_cal, kept_ref[...], swapped_ref[...])
    state = jnp.where(is_cal, swapped_ref[...], state_ref[...])
    gains = smoothing * state + (1.0 - smoothing) * solved
    shift = (feeds - place * rows) % feeds
    gains_ref[...] = pltpu.roll(gains, shift, 1)[:, :rows]
    power = jnp.sum(gains * gains, axis=0, keepdims=True)
    mean_power = total(power) / feeds
    scale = jnp.sqrt((mean_power + epsilon) / (power + mean_power + epsilon))
    down = jnp.broadcast_to(pltpu.roll(scale, shift, 1)[:, :128], (128, 128)).T[:rows]
    down = jnp.concatenate([down] * (feeds // 128), 1)
    factor = down * scale
    mine = mine_ref[...]
    mirror = mirror_ref[...]
    out_ref[:, 0, :] = ((mine + mirror) * factor).astype(jnp.bfloat16)
    out_ref[:, 1, :] = ((mine - mirror) * factor).astype(jnp.bfloat16)


def rescale(place, cal, kept, swapped, state, mine, mirror):
    rows, feeds = mine.shape
    vm = pl.BlockSpec(memory_space=pltpu.VMEM)
    sm = pl.BlockSpec(memory_space=pltpu.SMEM)
    return pl.pallas_call(
        rescale_kernel,
        out_shape=(jax.ShapeDtypeStruct((4, rows), jnp.float32), jax.ShapeDtypeStruct((rows, 2, feeds), jnp.bfloat16)),
        in_specs=[sm, sm] + [vm] * 5,
        out_specs=(vm, vm),
        compiler_params=pltpu.CompilerParams(vmem_limit_bytes=40 << 20),
        name="rescale",
    )(place, cal, kept, swapped, state, mine, mirror)


def groups(mesh_shape_x, mesh_shape_z):
    along_x = [[x * mesh_shape_z + z for x in range(mesh_shape_x)] for z in range(mesh_shape_z)]
    along_z = [[x * mesh_shape_z + z for z in range(mesh_shape_z)] for x in range(mesh_shape_x)]
    return along_x, along_z


def exchange(value, which):
    return lax.all_to_all(value, "tm", 0, 0, axis_index_groups=which)


def swap_cores(value):
    count = lax.axis_size("chan")
    return lax.ppermute(value, "chan", [(i, i ^ 1) for i in range(count)])


def on_device(samples, feed_flags, cal_channel, gain_state):
    feeds = samples.shape[2]
    tm_count = lax.axis_size("tm")
    nx = nz = 4
    along_x, along_z = groups(nx, nz)
    rows = feeds // tm_count
    tm = lax.axis_index("tm")
    f32, bf16 = jnp.float32, jnp.bfloat16
    place = tm.reshape(1).astype(jnp.int32)
    own_state = gain_state[0].reshape(4, rows)
    other_state = swap_cores(own_state)
    packed, cal = gram(cal_channel, samples[0], feed_flags, samples.shape[3] * tm_count)
    packed, cal, own_state, other_state = lax.optimization_barrier((packed, cal, own_state, other_state))
    is_cal = cal[0] > 0
    odd = lax.axis_index("chan") % 2 == 1

    def with_cal():
        part = fold(exchange(packed.reshape(nx, nz * rows, feeds), along_x))
        mine = jnp.sum(exchange(part.reshape(nz, rows, feeds), along_z).astype(f32), axis=0)
        got = exchange(jnp.broadcast_to(mine.astype(bf16)[None], (nz, rows, feeds)), along_z)
        got = exchange(jnp.broadcast_to(got.reshape(1, nz * rows, feeds), (nx, nz * rows, feeds)), along_x)
        solved, mirror = solve(place, got.reshape(feeds, feeds), rows)
        return solved, jnp.zeros((4, feeds), f32), mine, mirror

    def around_x(value):
        here = tm // nz
        got = [lax.dynamic_index_in_dim(value, here, 0, keepdims=False)]
        for shift in range(1, nx):
            pairs = [(i, (i + shift * nz) % tm_count) for i in range(tm_count)]
            block = lax.dynamic_index_in_dim(value, (here + shift) % nx, 0, keepdims=False)
            got.append(lax.ppermute(block, "tm", pairs))
        return jnp.stack(got)

    def without():
        blocks = packed.reshape(nx, nz * rows, feeds)
        lead = lax.cond(odd, around_x, lambda value: exchange(value, along_x), blocks[:, :FIRST])
        lead, trail = lax.optimization_barrier((lead, blocks[:, FIRST:]))
        part = fold(lead, exchange(trail, along_x))
        mine = jnp.sum(exchange(part.reshape(nz, rows, feeds), along_z).astype(f32), axis=0)
        states = jnp.concatenate([own_state, other_state], 0)
        high = states.astype(bf16)
        low = (states - high.astype(f32)).astype(bf16)
        halves = jnp.broadcast_to(jnp.concatenate([high, low], 0)[None], (tm_count, 16, rows))
        mirror = mine.astype(bf16).T.reshape(tm_count, rows, rows)
        got = exchange(jnp.concatenate([mirror, halves], 1), None)
        got = got.transpose(1, 0, 2).reshape(rows + 16, feeds).astype(f32)
        mirror, halves = got[:rows], got[rows:]
        states = halves[:8] + halves[8:]
        return states[4:], states[:4], mine, mirror

    kept, held, mine, mirror = lax.cond(is_cal, with_cal, without)
    gains, calibrated = rescale(place, cal, kept, swap_cores(kept), held, mine, mirror)
    return (calibrated[None], gains.reshape(1, 2, 2, rows))


def solution(mesh):
    return jax.shard_map(
        on_device,
        mesh=mesh,
        in_specs=(P("chan", None, None, "tm"), P("chan", None), P(), P("chan", None, None, "tm")),
        out_specs=(P("chan", "tm", None, None), P("chan", None, None, "tm")),
        check_vma=False,
    )
```

```python
import functools, math
import numpy as np
import jax
import jax.numpy as jnp
from jax import lax
from jax.experimental import pallas as pl
from jax.experimental.pallas import tpu as pltpu
from jax.sharding import PartitionSpec as P

ITERS = 8
FIRST = 32
epsilon = 1e-06
smoothing = 0.75

def gram_kernel(scale, cal_hbm, samples_hbm, flags_hbm, out_ref, is_cal_ref, cal_ref, samples_ref, flags_ref, left,
                right, sems):
    feeds, width = samples_ref.shape[1:]
    block = out_ref.shape[0]
    step = pl.program_id(0)

    @pl.when(step == 0)
    def _():
        copies = [
            pltpu.make_async_copy(cal_hbm, cal_ref, sems.at[0]),
            pltpu.make_async_copy(flags_hbm, flags_ref, sems.at[1]),
            pltpu.make_async_copy(samples_hbm.at[0], samples_ref.at[0], sems.at[2]),
            pltpu.make_async_copy(samples_hbm.at[1], samples_ref.at[1], sems.at[3]),
        ]
        for copy in copies:
            copy.start()
        copies[0].wait()
        chan = lax.axis_index("chan")
        is_cal_ref[0] = (cal_ref[chan // 2] == chan).astype(jnp.int32)
        copies[1].wait()
        good = jnp.broadcast_to(flags_ref[...].astype(jnp.float32), (128, feeds)).T
        good = jnp.concatenate([good] * (width // 128), 1)
        copies[2].wait()
        re = samples_ref[0].astype(jnp.float32) * good
        left[:, :width] = re.astype(jnp.bfloat16)
        copies[3].wait()
        im = samples_ref[1].astype(jnp.float32) * good
        left[:, width:] = im.astype(jnp.bfloat16)
        right[:, :width] = (re - im).astype(jnp.bfloat16)
        right[:, width:] = (re + im).astype(jnp.bfloat16)

    rows = pl.ds(pl.multiple_of(step * block, block), block)
    nt = (((1,), (1,)), ((), ()))
    both = lax.dot_general(left[rows, :], right[...], nt, preferred_element_type=jnp.float32)
    out_ref[...] = (both * scale).astype(jnp.bfloat16)


def gram(cal_channel, samples, flags, all_time):
    _, feeds, width = samples.shape
    blocks = 4
    bf16 = jnp.bfloat16
    anywhere = pl.BlockSpec(memory_space=pl.ANY)
    return pl.pallas_call(
        functools.partial(gram_kernel, 0.5 / all_time),
        grid=(blocks,),
        out_shape=(jax.ShapeDtypeStruct((feeds, feeds), bf16), jax.ShapeDtypeStruct((1,), jnp.int32)),
        in_specs=[anywhere] * 3,
        out_specs=(
            pl.BlockSpec((feeds // blocks, feeds), lambda i: (i, 0)),
            pl.BlockSpec(memory_space=pltpu.SMEM),
        ),
        scratch_shapes=[
            pltpu.SMEM(cal_channel.shape, jnp.int32),
            pltpu.VMEM(samples.shape, bf16),
            pltpu.VMEM(flags.shape, jnp.int32),
            pltpu.VMEM((feeds, 2 * width), bf16),
            pltpu.VMEM((feeds, 2 * width), bf16),
            pltpu.SemaphoreType.DMA((4,)),
        ],
        compiler_params=pltpu.CompilerParams(vmem_limit_bytes=56 << 20),
        name="gram",
    )(cal_channel, samples, flags)


def fold_kernel(*refs):
    *part_refs, out_ref = refs
    at = 0
    for ref in part_refs:
        rows = ref.shape[1]
        for first in range(0, rows, 16):
            parts = [ref[k, first:first + 16, :].astype(jnp.float32) for k in range(4)]
            total_rows = (parts[0] + parts[1]) + (parts[2] + parts[3])
            out_ref[at + first:at + first + 16, :] = total_rows.astype(jnp.bfloat16)
        at += rows


def fold(*pieces):
    feeds = pieces[0].shape[2]
    rows = sum(piece.shape[1] for piece in pieces)
    vm = pl.BlockSpec(memory_space=pltpu.VMEM)
    return pl.pallas_call(
        fold_kernel,
        out_shape=jax.ShapeDtypeStruct((rows, feeds), jnp.bfloat16),
        in_specs=[vm] * len(pieces),
        out_specs=vm,
        compiler_params=pltpu.CompilerParams(vmem_limit_bytes=40 << 20),
        name="fold",
    )(*pieces)


def basis_rows(feeds):
    f = np.arange(feeds, dtype=np.float64)
    ang = 2 * np.pi * np.arange(1, 3)[:, None] * f / feeds
    return (np.concatenate([np.cos(ang), np.sin(ang)]) / math.sqrt(feeds)).astype(np.float32)

def split3(v):
    hi = v.astype(jnp.bfloat16)
    rest = v - hi.astype(jnp.float32)
    mid = rest.astype(jnp.bfloat16)
    lo = (rest - mid.astype(jnp.float32)).astype(jnp.bfloat16)
    return hi, mid, lo

def total(v):
    return jnp.sum(v, axis=1, keepdims=True)

def solve_kernel(place_ref, own_ref, basis_ref, solved_ref, mirror_ref, mat_t):
    feeds = own_ref.shape[0]
    rows = mirror_ref.shape[0]
    for i in range(feeds // 256):
        mat_t[:, 256 * i:256 * (i + 1)] = own_ref[256 * i:256 * (i + 1), :].T
    mirror_ref[...] = mat_t[pl.ds(pl.multiple_of(place_ref[0] * rows, rows), rows), :].astype(jnp.float32)

    def sweep(_, carry):
        qr, qi, _, _ = carry
        s4 = jnp.concatenate([qr + qi, qr - qi], 0)
        hi, mid, lo = split3(s4)
        left = jnp.concatenate([hi, mid, lo, jnp.zeros_like(hi)], 0)
        with_t = jnp.dot(left, mat_t[...], preferred_element_type=jnp.float32)
        with_m = jnp.dot(left, own_ref[...], preferred_element_type=jnp.float32)
        with_t = (with_t[0:4] + with_t[4:8]) + with_t[8:12]
        with_m = (with_m[0:4] + with_m[4:8]) + with_m[8:12]
        zr = with_t[2:4] + with_m[0:2]
        zi = with_t[0:2] - with_m[2:4]
        one_r, two_r = zr[0:1], zr[1:2]
        one_i, two_i = zi[0:1], zi[1:2]
        n1 = total(one_r * one_r + one_i * one_i)
        cr = total(one_r * two_r + one_i * two_i)
        ci = total(one_r * two_i - one_i * two_r)
        square = epsilon + n1
        inverse = lax.rsqrt(square)
        first = square * inverse
        cr = cr / square
        ci = ci / square
        rest_r = two_r - (one_r * cr - one_i * ci)
        rest_i = two_i - (one_r * ci + one_i * cr)
        square_two = epsilon + total(rest_r * rest_r + rest_i * rest_i)
        inverse_two = lax.rsqrt(square_two)
        second = square_two * inverse_two
        qr = jnp.concatenate([one_r * inverse, rest_r * inverse_two], 0)
        qi = jnp.concatenate([one_i * inverse, rest_i * inverse_two], 0)
        return qr, qi, first, second

    one = jnp.ones((1, 1), jnp.float32)
    qr, qi, first, second = lax.fori_loop(0, ITERS, sweep, (basis_ref[0:2], basis_ref[2:4], one, one))
    weights = jnp.concatenate([jnp.sqrt(first * feeds), jnp.sqrt(second * feeds)], 0)
    solved_ref[...] = jnp.concatenate([qr * weights, qi * weights], 0)


def solve(place, own, rows):
    feeds = own.shape[1]
    vm = pl.BlockSpec(memory_space=pltpu.VMEM)
    return pl.pallas_call(
        solve_kernel,
        out_shape=(jax.ShapeDtypeStruct((4, feeds), jnp.float32), jax.ShapeDtypeStruct((rows, feeds), jnp.float32)),
        in_specs=[pl.BlockSpec(memory_space=pltpu.SMEM), vm, vm],
        out_specs=(vm, vm),
        scratch_shapes=[pltpu.VMEM((feeds, feeds), jnp.bfloat16)],
        compiler_params=pltpu.CompilerParams(vmem_limit_bytes=40 << 20),
        name="solve",
    )(place, own, jnp.asarray(basis_rows(feeds)))


def rescale_kernel(place_ref, cal_ref, kept_ref, swapped_ref, state_ref, mine_ref, mirror_ref,
                   gains_ref, out_ref):
    feeds = mine_ref.shape[1]
    rows = mine_ref.shape[0]
    place = place_ref[0]
    is_cal = cal_ref[0] > 0
    solved = jnp.where(is_cal, kept_ref[...], swapped_ref[...])
    state = jnp.where(is_cal, swapped_ref[...], state_ref[...])
    gains = smoothing * state + (1.0 - smoothing) * solved
    shift = (feeds - place * rows) % feeds
    gains_ref[...] = pltpu.roll(gains, shift, 1)[:, :rows]
    power = jnp.sum(gains * gains, axis=0, keepdims=True)
    mean_power = total(power) / feeds
    scale = jnp.sqrt((mean_power + epsilon) / (power + mean_power + epsilon))
    down = jnp.broadcast_to(pltpu.roll(scale, shift, 1)[:, :128], (128, 128)).T[:rows]
    down = jnp.concatenate([down] * (feeds // 128), 1)
    factor = down * scale
    mine = mine_ref[...]
    mirror = mirror_ref[...]
    out_ref[:, 0, :] = ((mine + mirror) * factor).astype(jnp.bfloat16)
    out_ref[:, 1, :] = ((mine - mirror) * factor).astype(jnp.bfloat16)


def rescale(place, cal, kept, swapped, state, mine, mirror):
    rows, feeds = mine.shape
    vm = pl.BlockSpec(memory_space=pltpu.VMEM)
    sm = pl.BlockSpec(memory_space=pltpu.SMEM)
    return pl.pallas_call(
        rescale_kernel,
        out_shape=(jax.ShapeDtypeStruct((4, rows), jnp.float32), jax.ShapeDtypeStruct((rows, 2, feeds), jnp.bfloat16)),
        in_specs=[sm, sm] + [vm] * 5,
        out_specs=(vm, vm),
        compiler_params=pltpu.CompilerParams(vmem_limit_bytes=40 << 20),
        name="rescale",
    )(place, cal, kept, swapped, state, mine, mirror)


def groups(mesh_shape_x, mesh_shape_z):
    along_x = [[x * mesh_shape_z + z for x in range(mesh_shape_x)] for z in range(mesh_shape_z)]
    along_z = [[x * mesh_shape_z + z for z in range(mesh_shape_z)] for x in range(mesh_shape_x)]
    return along_x, along_z


def exchange(value, which):
    return lax.all_to_all(value, "tm", 0, 0, axis_index_groups=which)


def swap_cores(value):
    count = lax.axis_size("chan")
    return lax.ppermute(value, "chan", [(i, i ^ 1) for i in range(count)])


def on_device(samples, feed_flags, cal_channel, gain_state):
    feeds = samples.shape[2]
    tm_count = lax.axis_size("tm")
    nx = nz = 4
    along_x, along_z = groups(nx, nz)
    rows = feeds // tm_count
    tm = lax.axis_index("tm")
    f32, bf16 = jnp.float32, jnp.bfloat16
    place = tm.reshape(1).astype(jnp.int32)
    own_state = gain_state[0].reshape(4, rows)
    other_state = swap_cores(own_state)
    packed, cal = gram(cal_channel, samples[0], feed_flags, samples.shape[3] * tm_count)
    packed, cal, own_state, other_state = lax.optimization_barrier((packed, cal, own_state, other_state))
    is_cal = cal[0] > 0
    odd = lax.axis_index("chan") % 2 == 1

    def with_cal():
        part = fold(exchange(packed.reshape(nx, nz * rows, feeds), along_x))
        mine = jnp.sum(exchange(part.reshape(nz, rows, feeds), along_z).astype(f32), axis=0)
        got = exchange(jnp.broadcast_to(mine.astype(bf16)[None], (nz, rows, feeds)), along_z)
        got = exchange(jnp.broadcast_to(got.reshape(1, nz * rows, feeds), (nx, nz * rows, feeds)), along_x)
        solved, mirror = solve(place, got.reshape(feeds, feeds), rows)
        return solved, jnp.zeros((4, feeds), f32), mine, mirror

    def around_x(value):
        here = tm // nz
        got = [lax.dynamic_index_in_dim(value, here, 0, keepdims=False)]
        for shift in range(1, nx):
            pairs = [(i, (i + shift * nz) % tm_count) for i in range(tm_count)]
            block = lax.dynamic_index_in_dim(value, (here + shift) % nx, 0, keepdims=False)
            got.append(lax.ppermute(block, "tm", pairs))
        return jnp.stack(got)

    def without():
        blocks = packed.reshape(nx, nz * rows, feeds)
        lead = lax.cond(odd, around_x, lambda value: exchange(value, along_x), blocks[:, :FIRST])
        lead, trail = lax.optimization_barrier((lead, blocks[:, FIRST:]))
        part = fold(lead, exchange(trail, along_x))
        mine = jnp.sum(exchange(part.reshape(nz, rows, feeds), along_z).astype(f32), axis=0)
        states = jnp.concatenate([own_state, other_state], 0)
        high = states.astype(bf16)
        low = (states - high.astype(f32)).astype(bf16)
        halves = jnp.broadcast_to(jnp.concatenate([high, low], 0)[None], (tm_count, 16, rows))
        mirror = mine.astype(bf16).T.reshape(tm_count, rows, rows)
        got = exchange(jnp.concatenate([mirror, halves], 1), None)
        got = got.transpose(1, 0, 2).reshape(rows + 16, feeds).astype(f32)
        mirror, halves = got[:rows], got[rows:]
        states = halves[:8] + halves[8:]
        return states[4:], states[:4], mine, mirror

    kept, held, mine, mirror = lax.cond(is_cal, with_cal, without)
    gains, calibrated = rescale(place, cal, kept, swap_cores(kept), held, mine, mirror)
    return (calibrated[None], gains.reshape(1, 2, 2, rows))


def solution(mesh):
    return jax.shard_map(
        on_device,
        mesh=mesh,
        in_specs=(P("chan", None, None, "tm"), P("chan", None), P(), P("chan", None, None, "tm")),
        out_specs=(P("chan", "tm", None, None), P("chan", None, None, "tm")),
        check_vma=False,
    )
```

```python
import functools, math
import numpy as np
import jax
import jax.numpy as jnp
from jax import lax
from jax.experimental import pallas as pl
from jax.experimental.pallas import tpu as pltpu
from jax.sharding import PartitionSpec as P

ITERS = 8
FIRST = 16
epsilon = 1e-06
smoothing = 0.75

def gram_kernel(scale, cal_hbm, samples_hbm, flags_hbm, out_ref, is_cal_ref, cal_ref, samples_ref, flags_ref, left,
                right, sems):
    feeds, width = samples_ref.shape[1:]
    block = out_ref.shape[0]
    step = pl.program_id(0)

    @pl.when(step == 0)
    def _():
        copies = [
            pltpu.make_async_copy(cal_hbm, cal_ref, sems.at[0]),
            pltpu.make_async_copy(flags_hbm, flags_ref, sems.at[1]),
            pltpu.make_async_copy(samples_hbm.at[0], samples_ref.at[0], sems.at[2]),
            pltpu.make_async_copy(samples_hbm.at[1], samples_ref.at[1], sems.at[3]),
        ]
        for copy in copies:
            copy.start()
        copies[0].wait()
        chan = lax.axis_index("chan")
        is_cal_ref[0] = (cal_ref[chan // 2] == chan).astype(jnp.int32)
        copies[1].wait()
        good = jnp.broadcast_to(flags_ref[...].astype(jnp.float32), (128, feeds)).T
        good = jnp.concatenate([good] * (width // 128), 1)
        copies[2].wait()
        re = samples_ref[0].astype(jnp.float32) * good
        left[:, :width] = re.astype(jnp.bfloat16)
        copies[3].wait()
        im = samples_ref[1].astype(jnp.float32) * good
        left[:, width:] = im.astype(jnp.bfloat16)
        right[:, :width] = (re - im).astype(jnp.bfloat16)
        right[:, width:] = (re + im).astype(jnp.bfloat16)

    rows = pl.ds(pl.multiple_of(step * block, block), block)
    nt = (((1,), (1,)), ((), ()))
    both = lax.dot_general(left[rows, :], right[...], nt, preferred_element_type=jnp.float32)
    out_ref[...] = (both * scale).astype(jnp.bfloat16)


def gram(cal_channel, samples, flags, all_time):
    _, feeds, width = samples.shape
    blocks = 4
    bf16 = jnp.bfloat16
    anywhere = pl.BlockSpec(memory_space=pl.ANY)
    return pl.pallas_call(
        functools.partial(gram_kernel, 0.5 / all_time),
        grid=(blocks,),
        out_shape=(jax.ShapeDtypeStruct((feeds, feeds), bf16), jax.ShapeDtypeStruct((1,), jnp.int32)),
        in_specs=[anywhere] * 3,
        out_specs=(
            pl.BlockSpec((feeds // blocks, feeds), lambda i: (i, 0)),
            pl.BlockSpec(memory_space=pltpu.SMEM),
        ),
        scratch_shapes=[
            pltpu.SMEM(cal_channel.shape, jnp.int32),
            pltpu.VMEM(samples.shape, bf16),
            pltpu.VMEM(flags.shape, jnp.int32),
            pltpu.VMEM((feeds, 2 * width), bf16),
            pltpu.VMEM((feeds, 2 * width), bf16),
            pltpu.SemaphoreType.DMA((4,)),
        ],
        compiler_params=pltpu.CompilerParams(vmem_limit_bytes=56 << 20),
        name="gram",
    )(cal_channel, samples, flags)


def fold_kernel(*refs):
    *part_refs, out_ref = refs
    at = 0
    for ref in part_refs:
        rows = ref.shape[1]
        for first in range(0, rows, 16):
            parts = [ref[k, first:first + 16, :].astype(jnp.float32) for k in range(4)]
            total_rows = (parts[0] + parts[1]) + (parts[2] + parts[3])
            out_ref[at + first:at + first + 16, :] = total_rows.astype(jnp.bfloat16)
        at += rows


def fold(*pieces):
    feeds = pieces[0].shape[2]
    rows = sum(piece.shape[1] for piece in pieces)
    vm = pl.BlockSpec(memory_space=pltpu.VMEM)
    return pl.pallas_call(
        fold_kernel,
        out_shape=jax.ShapeDtypeStruct((rows, feeds), jnp.bfloat16),
        in_specs=[vm] * len(pieces),
        out_specs=vm,
        compiler_params=pltpu.CompilerParams(vmem_limit_bytes=40 << 20),
        name="fold",
    )(*pieces)


def basis_rows(feeds):
    f = np.arange(feeds, dtype=np.float64)
    ang = 2 * np.pi * np.arange(1, 3)[:, None] * f / feeds
    return (np.concatenate([np.cos(ang), np.sin(ang)]) / math.sqrt(feeds)).astype(np.float32)

def split3(v):
    hi = v.astype(jnp.bfloat16)
    rest = v - hi.astype(jnp.float32)
    mid = rest.astype(jnp.bfloat16)
    lo = (rest - mid.astype(jnp.float32)).astype(jnp.bfloat16)
    return hi, mid, lo

def total(v):
    return jnp.sum(v, axis=1, keepdims=True)

def solve_kernel(place_ref, own_ref, basis_ref, solved_ref, mirror_ref, mat_t):
    feeds = own_ref.shape[0]
    rows = mirror_ref.shape[0]
    for i in range(feeds // 256):
        mat_t[:, 256 * i:256 * (i + 1)] = own_ref[256 * i:256 * (i + 1), :].T
    mirror_ref[...] = mat_t[pl.ds(pl.multiple_of(place_ref[0] * rows, rows), rows), :]

    def sweep(_, carry):
        qr, qi, _, _ = carry
        s4 = jnp.concatenate([qr + qi, qr - qi], 0)
        hi, mid, lo = split3(s4)
        left = jnp.concatenate([hi, mid, lo, jnp.zeros_like(hi)], 0)
        with_t = jnp.dot(left, mat_t[...], preferred_element_type=jnp.float32)
        with_m = jnp.dot(left, own_ref[...], preferred_element_type=jnp.float32)
        with_t = (with_t[0:4] + with_t[4:8]) + with_t[8:12]
        with_m = (with_m[0:4] + with_m[4:8]) + with_m[8:12]
        zr = with_t[2:4] + with_m[0:2]
        zi = with_t[0:2] - with_m[2:4]
        one_r, two_r = zr[0:1], zr[1:2]
        one_i, two_i = zi[0:1], zi[1:2]
        n1 = total(one_r * one_r + one_i * one_i)
        cr = total(one_r * two_r + one_i * two_i)
        ci = total(one_r * two_i - one_i * two_r)
        square = epsilon + n1
        inverse = lax.rsqrt(square)
        first = square * inverse
        cr = cr / square
        ci = ci / square
        rest_r = two_r - (one_r * cr - one_i * ci)
        rest_i = two_i - (one_r * ci + one_i * cr)
        square_two = epsilon + total(rest_r * rest_r + rest_i * rest_i)
        inverse_two = lax.rsqrt(square_two)
        second = square_two * inverse_two
        qr = jnp.concatenate([one_r * inverse, rest_r * inverse_two], 0)
        qi = jnp.concatenate([one_i * inverse, rest_i * inverse_two], 0)
        return qr, qi, first, second

    one = jnp.ones((1, 1), jnp.float32)
    qr, qi, first, second = lax.fori_loop(0, ITERS, sweep, (basis_ref[0:2], basis_ref[2:4], one, one))
    weights = jnp.concatenate([jnp.sqrt(first * feeds), jnp.sqrt(second * feeds)], 0)
    solved_ref[...] = jnp.concatenate([qr * weights, qi * weights], 0)


def solve(place, own, rows):
    feeds = own.shape[1]
    vm = pl.BlockSpec(memory_space=pltpu.VMEM)
    return pl.pallas_call(
        solve_kernel,
        out_shape=(jax.ShapeDtypeStruct((4, feeds), jnp.float32), jax.ShapeDtypeStruct((rows, feeds), jnp.bfloat16)),
        in_specs=[pl.BlockSpec(memory_space=pltpu.SMEM), vm, vm],
        out_specs=(vm, vm),
        scratch_shapes=[pltpu.VMEM((feeds, feeds), jnp.bfloat16)],
        compiler_params=pltpu.CompilerParams(vmem_limit_bytes=40 << 20),
        name="solve",
    )(place, own, jnp.asarray(basis_rows(feeds)))


def rescale_kernel(place_ref, cal_ref, kept_ref, swapped_ref, state_ref, mine_ref, mirror_ref,
                   gains_ref, out_ref):
    feeds = mine_ref.shape[1]
    rows = mine_ref.shape[0]
    place = place_ref[0]
    is_cal = cal_ref[0] > 0
    solved = jnp.where(is_cal, kept_ref[...], swapped_ref[...])
    state = jnp.where(is_cal, swapped_ref[...], state_ref[...])
    gains = smoothing * state + (1.0 - smoothing) * solved
    shift = (feeds - place * rows) % feeds
    gains_ref[...] = pltpu.roll(gains, shift, 1)[:, :rows]
    power = jnp.sum(gains * gains, axis=0, keepdims=True)
    mean_power = total(power) / feeds
    scale = jnp.sqrt((mean_power + epsilon) / (power + mean_power + epsilon))
    down = jnp.broadcast_to(pltpu.roll(scale, shift, 1)[:, :128], (128, 128)).T[:rows]
    down = jnp.concatenate([down] * (feeds // 128), 1)
    factor = down * scale
    mine = mine_ref[...].astype(jnp.float32)
    mirror = mirror_ref[...].astype(jnp.float32)
    out_ref[:, 0, :] = ((mine + mirror) * factor).astype(jnp.bfloat16)
    out_ref[:, 1, :] = ((mine - mirror) * factor).astype(jnp.bfloat16)


def rescale(place, cal, kept, swapped, state, mine, mirror):
    rows, feeds = mine.shape
    vm = pl.BlockSpec(memory_space=pltpu.VMEM)
    sm = pl.BlockSpec(memory_space=pltpu.SMEM)
    return pl.pallas_call(
        rescale_kernel,
        out_shape=(jax.ShapeDtypeStruct((4, rows), jnp.float32), jax.ShapeDtypeStruct((rows, 2, feeds), jnp.bfloat16)),
        in_specs=[sm, sm] + [vm] * 5,
        out_specs=(vm, vm),
        compiler_params=pltpu.CompilerParams(vmem_limit_bytes=40 << 20),
        name="rescale",
    )(place, cal, kept, swapped, state, mine, mirror)


def groups(mesh_shape_x, mesh_shape_z):
    along_x = [[x * mesh_shape_z + z for x in range(mesh_shape_x)] for z in range(mesh_shape_z)]
    along_z = [[x * mesh_shape_z + z for z in range(mesh_shape_z)] for x in range(mesh_shape_x)]
    return along_x, along_z


def exchange(value, which):
    return lax.all_to_all(value, "tm", 0, 0, axis_index_groups=which)


def swap_cores(value):
    count = lax.axis_size("chan")
    return lax.ppermute(value, "chan", [(i, i ^ 1) for i in range(count)])


def on_device(samples, feed_flags, cal_channel, gain_state):
    feeds = samples.shape[2]
    tm_count = lax.axis_size("tm")
    nx = nz = 4
    along_x, along_z = groups(nx, nz)
    rows = feeds // tm_count
    tm = lax.axis_index("tm")
    f32, bf16 = jnp.float32, jnp.bfloat16
    place = tm.reshape(1).astype(jnp.int32)
    own_state = gain_state[0].reshape(4, rows)
    other_state = swap_cores(own_state)
    packed, cal = gram(cal_channel, samples[0], feed_flags, samples.shape[3] * tm_count)
    packed, cal, own_state, other_state = lax.optimization_barrier((packed, cal, own_state, other_state))
    is_cal = cal[0] > 0
    odd = lax.axis_index("chan") % 2 == 1

    def with_cal():
        part = fold(exchange(packed.reshape(nx, nz * rows, feeds), along_x))
        mine = fold(exchange(part.reshape(nz, rows, feeds), along_z))
        got = exchange(jnp.broadcast_to(mine[None], (nz, rows, feeds)), along_z)
        got = exchange(jnp.broadcast_to(got.reshape(1, nz * rows, feeds), (nx, nz * rows, feeds)), along_x)
        solved, mirror = solve(place, got.reshape(feeds, feeds), rows)
        return solved, jnp.zeros((4, feeds), f32), mine, mirror

    def around_x(value):
        here = tm // nz
        got = [lax.dynamic_index_in_dim(value, here, 0, keepdims=False)]
        for shift in range(1, nx):
            pairs = [(i, (i + shift * nz) % tm_count) for i in range(tm_count)]
            block = lax.dynamic_index_in_dim(value, (here + shift) % nx, 0, keepdims=False)
            got.append(lax.ppermute(block, "tm", pairs))
        return jnp.stack(got)

    def without():
        blocks = packed.reshape(nx, nz * rows, feeds)
        lead = lax.cond(odd, around_x, lambda value: exchange(value, along_x), blocks[:, :FIRST])
        lead, trail = lax.optimization_barrier((lead, blocks[:, FIRST:]))
        part = fold(lead, exchange(trail, along_x))
        mine = fold(exchange(part.reshape(nz, rows, feeds), along_z))
        states = jnp.concatenate([own_state, other_state], 0)
        high = states.astype(bf16)
        low = (states - high.astype(f32)).astype(bf16)
        halves = jnp.broadcast_to(jnp.concatenate([high, low], 0)[None], (tm_count, 16, rows))
        mirror = mine.T.reshape(tm_count, rows, rows)
        got = exchange(jnp.concatenate([mirror, halves], 1), None)
        got = got.transpose(1, 0, 2).reshape(rows + 16, feeds)
        mirror, halves = got[:rows], got[rows:].astype(f32)
        states = halves[:8] + halves[8:]
        return states[4:], states[:4], mine, mirror

    kept, held, mine, mirror = lax.cond(is_cal, with_cal, without)
    gains, calibrated = rescale(place, cal, kept, swap_cores(kept), held, mine, mirror)
    return (calibrated[None], gains.reshape(1, 2, 2, rows))


def solution(mesh):
    return jax.shard_map(
        on_device,
        mesh=mesh,
        in_specs=(P("chan", None, None, "tm"), P("chan", None), P(), P("chan", None, None, "tm")),
        out_specs=(P("chan", "tm", None, None), P("chan", None, None, "tm")),
        check_vma=False,
    )
```
